32 devices in a mesh: groups: 2 (over x), depth: 16 (over z, y, core).
Axes of the slice: x: 2, y: 2, z: 4, core: 2. Of those that a mesh axis runs over, the one named last changes fastest.
Arguments:
- fields: float32 [32, 2, 2, 512, 256], P(('groups', 'depth')), parts along dimension 0, may hold values from -6 to 6
- vel_tiles: float32 [64, 128, 128], P(('groups', 'depth')), parts along dimension 0, may hold values from 0.5 to 2
- tile_ids: int32 [32, 2, 4, 2], P(('groups', 'depth')), parts along dimension 0, may hold values from 0 to 31
- orders: int32 [32, 2], P(('groups', 'depth')), parts along dimension 0, may hold values from 1 to 3
- term_weights: float32 [3], replicated, may hold values from 0.05 to 0.12
- phase_rates: float32 [4], replicated, may hold values from 1 to 4
- owners: int32 [32, 16], P(('groups', 'depth')), parts along dimension 0, may hold values from 0 to 15, as said below
- image_slots: int32 [32, 16], P(('groups', 'depth')), parts along dimension 0, may hold values from 0 to 7
Outputs:
- image_volume: float32 [256, 128, 128], P(('groups', 'depth')), parts along dimension 0
- wavefields_out: float32 [32, 2, 2, 512, 256], P(('groups', 'depth')), parts along dimension 0
The draws below stay inside these ranges and needn't reach their ends.
There are 2 independent parts, one for each index of `groups`. The reference program is written for one: setup_inputs(seed, part) draws one part's arguments, and reference() takes and returns one part's arrays. A program takes and returns all parts, laid end to end along the dimension named above; an argument that names none is the same for every part. Nothing has to cross between parts.
Inputs may be any that keep to these rules, and one draw needn't show every extreme that they name: `owners`: of the 16 tiles of one slab, at most 2 have the same owner, and some owner gets exactly 2 of them.
All inputs are finite; a program needn't handle non-finite values.
Results may differ from the reference program's by a relative error of at most 0.0003.
Values sent between devices are 32-bit elements; how exact they have to be, the bound alone decides.
No kernel may reach another device: no remote copies, remote signals or barrier semaphores. Data moves between devices by JAX's collectives and lax.ppermute only.
A program may use at most 64 MiB of HBM per device.

```python
import math
import jax
import jax.numpy as jnp

NX = 512
NY = 256
TS = 128
TICKS = 2
STEPS = 2
ORDER = 3
CAP = 2
IMG_SLOTS = 8
SECTIONS = 16
VTILES = 32
TX = 4
TY = 2
PIECES = 16


def draw_owners(key, part):

    def draw_slab(slab_index):
        slab_key = jax.random.fold_in(jax.random.fold_in(key, 7), slab_index)
        key_full, key_order, key_shuffle = jax.random.split(slab_key, 3)
        seat_total = SECTIONS * CAP
        full_owner = jax.random.randint(key_full, (), 0, SECTIONS)
        seat_rank = jnp.argsort(jax.random.permutation(key_order, seat_total))
        seats_all = jnp.arange(seat_total)
        scores = seat_rank + jnp.where(seats_all // CAP == full_owner, 0, seat_total)
        chosen = jnp.argsort(scores)[:PIECES]
        owner_list = (chosen // CAP).astype(jnp.int32)
        return owner_list[jax.random.permutation(key_shuffle, PIECES)]
    return jax.vmap(draw_slab)(jnp.arange(SECTIONS)).astype(jnp.int32)


def touch_ends(entries, key, smallest, top_value):
    index_at = [jax.random.randint(jax.random.fold_in(key, axis), (), 0, length) for axis, length in enumerate(entries.shape)]
    main_axis = entries.shape.index(max(entries.shape))
    next_to = index_at[:main_axis] + [(index_at[main_axis] + 1) % entries.shape[main_axis]] + index_at[main_axis + 1:]
    return entries.at[tuple(index_at)].set(smallest).at[tuple(next_to)].set(top_value)


def steps_of(own_key, dims, shards, low, largest):
    def one(axis_at, blocks):
        heights = jax.random.uniform(jax.random.fold_in(jax.random.fold_in(own_key, 6), axis_at), (blocks,), jnp.float32, low / len(shards), largest / len(shards))
        return jnp.repeat(jnp.exp(heights), dims[axis_at] // blocks).reshape((-1,) + (1,) * (len(dims) - axis_at - 1))

    factor_of = one(*shards[0])
    for cut in shards[1:]:
        factor_of = factor_of * one(*cut)
    return factor_of


def gaussian(own_key, shape, deviation, limit, shards=(), held_as=jnp.bfloat16):
    drawn = jax.random.normal(own_key, shape, jnp.float32) * deviation
    if len(shards) > 0:
        drawn = steps_of(own_key, shape, shards, -0.22, 0.18) * drawn
    return jnp.clip(drawn, min=-limit, max=limit).astype(held_as)


def setup_inputs(seed: int = 0, part: int = 0) -> dict:
    arg_keys = jax.random.split(jax.random.key(seed), 9)
    part_splits = jax.random.split(jax.random.fold_in(arg_keys[8], part), 9)
    return {
        "fields": gaussian(part_splits[0], (SECTIONS, 2, 2, NX, NY), 1.0, 6.0, ((0, 16),), jnp.float32),
        "vel_tiles": jnp.clip(jnp.exp(math.log(2.0) - 1.3862944 * jax.random.uniform(part_splits[1], (VTILES, TS, TS), jnp.float32) ** steps_of(part_splits[1], (VTILES, TS, TS), ((0, 16),), -0.2, 0.2)), 0.5, 2.0),
        "tile_ids": touch_ends(jax.random.randint(part_splits[2], (SECTIONS, STEPS, TX, TY), 0, VTILES), jax.random.fold_in(part_splits[2], 1), 0, VTILES - 1).astype(jnp.int32),
        "orders": touch_ends(jax.random.randint(part_splits[3], (SECTIONS, STEPS), 1, ORDER + 1), jax.random.fold_in(part_splits[3], 1), 1, ORDER).astype(jnp.int32),
        "term_weights": jnp.clip(jax.random.uniform(arg_keys[4], (ORDER,), jnp.float32, 0.05, 0.12), 0.05, 0.12),
        "phase_rates": jnp.clip(jax.random.uniform(arg_keys[5], (ORDER + 1,), jnp.float32, 1.0, 4.0), 1.0, 4.0),
        "owners": draw_owners(jax.random.fold_in(jax.random.fold_in(arg_keys[8], part), 71), part),
        "image_slots": touch_ends(jax.random.randint(part_splits[7], (SECTIONS, PIECES), 0, IMG_SLOTS), jax.random.fold_in(part_splits[7], 1), 0, IMG_SLOTS - 1).astype(jnp.int32),
    }


def mcclellan(fields_in):
    padded = jnp.pad(fields_in, ((0, 0), (1, 1), (1, 1)))
    beside = padded[:, 2:, 1:-1] + padded[:, :-2, 1:-1] + padded[:, 1:-1, 2:] + padded[:, 1:-1, :-2]
    corner = padded[:, 2:, 2:] + padded[:, :-2, :-2] + padded[:, 2:, :-2] + padded[:, :-2, 2:]
    return -0.5 * fields_in + 0.25 * beside + 0.125 * corner


def rotate_add(result, series_term, real_part, imag_part, pair_signs):
    pieces_out = []
    for pair_index, pair_sign in enumerate(pair_signs):
        real_in = series_term[2 * pair_index]
        imag_in = series_term[2 * pair_index + 1]
        pieces_out.append(result[2 * pair_index] + real_part * real_in - pair_sign * imag_part * imag_in)
        pieces_out.append(result[2 * pair_index + 1] + real_part * imag_in + pair_sign * imag_part * real_in)
    return jnp.stack(pieces_out)


def reference_step(wave_state, slowness_now, order_now, weights, phase_rates):
    result = jnp.zeros_like(wave_state)
    previous = wave_state
    current = wave_state
    for degree in range(ORDER + 1):
        if degree == 0:
            series_term = wave_state
        elif degree == 1:
            series_term = mcclellan(wave_state)
        else:
            series_term = 2.0 * mcclellan(current) - previous
        if degree >= 1:
            previous, current = current, series_term
        active = (degree <= order_now).astype(jnp.float32)
        angle_now = phase_rates[degree] * slowness_now
        real_part = weights[degree] * jnp.cos(angle_now) * active
        imag_part = weights[degree] * jnp.sin(angle_now) * active
        result = rotate_add(result, series_term, real_part, imag_part, (1.0, -1.0))
    return result


def reference(fields, vel_tiles, tile_ids, orders, term_weights, phase_rates, owners, image_slots):
    sections = fields.shape[0]
    cells_x = fields.shape[3]
    cells_y = fields.shape[4]
    picked = vel_tiles[tile_ids]
    slowness = picked.transpose(0, 1, 2, 4, 3, 5).reshape(sections, STEPS, cells_x, cells_y)
    weights = jnp.concatenate([(1.0 - jnp.sum(term_weights))[None], term_weights])
    wave_state = fields.reshape(sections, 4, cells_x, cells_y)
    image_sum = jnp.zeros((sections, STEPS, cells_x, cells_y), jnp.float32)
    stepper = jax.vmap(reference_step, in_axes=(0, 0, 0, None, None))
    for tick_index in range(TICKS):
        if tick_index > 0:
            wave_state = jnp.concatenate([jnp.zeros_like(wave_state[:1]), wave_state[:-1]], 0)
        for step_index in range(STEPS):
            wave_state = stepper(wave_state, slowness[:, step_index], orders[:, step_index], weights, phase_rates)
            product = wave_state[:, 0] * wave_state[:, 2] + wave_state[:, 1] * wave_state[:, 3]
            image_sum = image_sum.at[:, step_index].add(product)
    tile_rows = image_sum.reshape(sections, STEPS, TX, TS, TY, TS).transpose(0, 1, 2, 4, 3, 5)
    tile_rows = tile_rows.reshape(sections * PIECES, TS * TS)
    targets = (owners * IMG_SLOTS + image_slots).reshape(-1).astype(jnp.int32)
    volume = jax.ops.segment_sum(tile_rows, targets, num_segments=sections * IMG_SLOTS)
    return volume.reshape(sections * IMG_SLOTS, TS, TS), wave_state.reshape(fields.shape)
```

```python
from functools import partial

import jax
import jax.numpy as jnp
import numpy as np
from jax import lax
from jax.experimental import pallas as pl
from jax.experimental.pallas import tpu as pltpu
from jax.sharding import PartitionSpec as P

TICKS = 2
CAP = 2
IMG_SLOTS = 8
LANES = 128
SUBS = 8
VMEM = pl.BlockSpec(memory_space=pltpu.VMEM)
SMEM = pl.BlockSpec(memory_space=pltpu.SMEM)
ANY = pl.BlockSpec(memory_space=pl.ANY)
PARAMS = pltpu.CompilerParams(vmem_limit_bytes=56 * 2**20)


def in_powers(terms):
    rows = np.zeros((terms, terms))
    polys = [np.array([1.0]), np.array([-1.0, 1.0])]
    while len(polys) < terms:
        grown = np.convolve(polys[-1], [-2.0, 2.0])
        grown[: len(polys[-2])] -= polys[-2]
        polys.append(grown)
    for k in range(terms):
        rows[k, : len(polys[k])] = polys[k] / 8.0 ** np.arange(len(polys[k]))
    return rows


def fitted():
    nodes = 0.25 * (1.0 - np.cos((np.arange(400) + 0.5) * np.pi / 400)) / 2.0
    r = np.sqrt(nodes)
    sine = np.polynomial.chebyshev.Chebyshev.fit(nodes, np.sqrt(2.0) * np.sin(np.pi * r) / r, 4)
    cosine = np.polynomial.chebyshev.Chebyshev.fit(nodes, np.sqrt(2.0) * np.cos(np.pi * r), 4)
    make = np.polynomial.polynomial.Polynomial
    return (
        [float(c) for c in sine.convert(kind=make).coef],
        [float(c) for c in cosine.convert(kind=make).coef],
    )


SINE, COSINE = fitted()


def horner(x, coefs):
    out = coefs[-1] * x + coefs[-2]
    for c in coefs[-3::-1]:
        out = out * x + c
    return out


def cos_sin(turns):
    r = turns - jnp.round(turns)
    r2 = r * r
    s = r * horner(r2, SINE)
    c = horner(r2, COSINE)
    return 1.0 - s * s, s * c


def lanes_121(blocks):
    lane = lax.broadcasted_iota(jnp.int32, blocks[0].shape, 1)
    first, last = lane == 0, lane == LANES - 1
    turned = [pltpu.roll(b, 1, 1) for b in blocks]
    sums = [
        b + jnp.where(first, turned[i - 1] if i else 0.0, turned[i])
        for i, b in enumerate(blocks)
    ]
    back = [pltpu.roll(s, LANES - 1, 1) for s in sums]
    return [
        s + jnp.where(last, back[i + 1] if i + 1 < len(sums) else blocks[i], back[i])
        for i, s in enumerate(sums)
    ]


class Rows:
    def __init__(self, ref):
        self.ref = ref
        self.planes, padded, _, self.cells_y = ref.shape
        self.R = padded - 2
        self.blocks = self.cells_y // LANES

    def get(self, p, r):
        return [self.ref[p, r + 1, :, b * LANES : (b + 1) * LANES] for b in range(self.blocks)]

    def put(self, p, r, values):
        for b, v in enumerate(values):
            self.ref[p, r + 1, :, b * LANES : (b + 1) * LANES] = v

    def halo(self):
        for p in range(self.planes):
            for b in range(self.blocks):
                at = slice(b * LANES, (b + 1) * LANES)
                sub = lax.broadcasted_iota(jnp.int32, (SUBS, LANES), 0)
                low = pltpu.roll(self.ref[p, self.R, :, at], 1, 0)
                self.ref[p, 0, :, at] = jnp.where(sub == 0, 0.0, low)
                high = pltpu.roll(self.ref[p, 1, :, at], SUBS - 1, 0)
                self.ref[p, self.R + 1, :, at] = jnp.where(sub == SUBS - 1, 0.0, high)


def smoothed(src, unroll, visit):
    planes = range(src.planes)

    def body(r, carry):
        values, kept = [], []
        for p in planes:
            here, below = carry[p]
            nxt = src.get(p, r + 1)
            above = [n + h for n, h in zip(nxt, here)]
            values.append(lanes_121([a + b for a, b in zip(above, below)]))
            kept.append((nxt, above))
        visit(r, values)
        return kept

    start = []
    for p in planes:
        here, before = src.get(p, 0), src.get(p, -1)
        start.append((here, [h + b for h, b in zip(here, before)]))
    lax.fori_loop(0, src.R, body, start, unroll=unroll)


def depth_step(levels, coefs, signs, emit):
    for low, high in zip(levels[:-2], levels[1:-1]):

        def store(r, values, high=high):
            for p, v in enumerate(values):
                high.put(p, r, v)

        smoothed(low, 4, store)
        high.halo()

    def combine(r, values):
        result = [None] * len(values)
        terms = len(levels)
        for k in range(terms):
            for b in range(levels[0].blocks):
                at = slice(b * LANES, (b + 1) * LANES)
                a = coefs[2 * k, r, :, at]
                s = coefs[2 * k + 1, r, :, at]
                for pair, sign in enumerate(signs):
                    if k == terms - 1:
                        re, im = values[2 * pair][b], values[2 * pair + 1][b]
                    else:
                        re, im = (levels[k].get(2 * pair + i, r)[b] for i in (0, 1))
                    x, y = a * re, a * im
                    u, v = s * im, s * re
                    x, y = (x - u, y + v) if sign > 0 else (x + u, y - v)
                    for i, w in ((0, x), (1, y)):
                        slot = result[2 * pair + i] = result[2 * pair + i] or [None] * levels[0].blocks
                        slot[b] = w if slot[b] is None else slot[b] + w
        emit(r, result)

    smoothed(levels[-2], 2, combine)


def fetch(field_ref, flat, sem):
    copies = [
        pltpu.make_async_copy(field_ref.at[:, :, pl.ds(b * LANES, LANES)], flat.at[:, b], sem.at[b])
        for b in range(flat.shape[1])
    ]
    for copy in copies:
        copy.start()
    return copies


def load_rows(flat, state):
    def body(r, _):
        for p in range(state.planes):
            state.put(
                p, r, [flat[p, b, pl.ds(r, SUBS, stride=state.R), :] for b in range(state.blocks)]
            )
        return 0

    lax.fori_loop(0, state.R, body, 0, unroll=4)
    state.halo()


def product(source, receiver, b):
    return source[0][b] * receiver[0][b] + source[1][b] * receiver[1][b]


def coefs_kernel(
    axis, pieces, ids_ref, orders_ref, ids_up_ref, orders_up_ref, weights_ref, rates_ref, *rest
):
    tiles, (fields_ref, coefs_ref, image_ref), (library, slow, sems, flat, flat_sem, *levels) = (
        rest[: len(pieces)],
        rest[len(pieces) : len(pieces) + 3],
        rest[len(pieces) + 3 :],
    )
    arriving = fetch(fields_ref, flat, flat_sem)
    per = library.shape[0] // sum(len(at) for at in pieces)
    copies = []
    for ref, at in zip(tiles, pieces):
        for i, k in enumerate(at):
            source = ref.at[i] if len(at) > 1 else ref
            copies.append(
                pltpu.make_async_copy(source, library.at[pl.ds(k * per, per)], sems.at[len(copies)])
            )
            copies[-1].start()
    for copy in copies:
        copy.wait()
    me = lax.axis_index(axis)
    steps, tiles_x, tiles_y = ids_ref.shape[-3:]
    size = library.shape[1]
    terms = rates_ref.shape[0]
    powers = in_powers(terms)
    R = coefs_ref.shape[3]
    blocks = coefs_ref.shape[5] // LANES
    total = weights_ref[0]
    for k in range(1, terms - 1):
        total = total + weights_ref[k]
    base = [1.0 - total] + [weights_ref[k] for k in range(terms - 1)]
    turn = [rates_ref[k] * (0.5 / np.pi) for k in range(terms)]
    for which, (ids, orders) in enumerate(((ids_up_ref, orders_up_ref), (ids_ref, orders_ref))):
        for j in range(steps):
            for a in range(tiles_x):
                for b in range(tiles_y):
                    tile = ids[0, j, a, b]
                    at = (tile // per ^ me) * per + tile % per
                    slow[b, a * size : (a + 1) * size, :] = library[at]
            scale = [jnp.where(k <= orders[0, j], base[k], 0.0) for k in range(terms)]

            def body(r, _):
                for b in range(blocks):
                    at = slice(b * LANES, (b + 1) * LANES)
                    here = slow[b, pl.ds(r, SUBS, stride=R), :]
                    parts = []
                    for k in range(terms):
                        c, s = cos_sin(here * turn[k])
                        parts.append((c * scale[k], s * scale[k]))
                    for m in range(terms):
                        for i in (0, 1):
                            out = None
                            for k in range(m, terms):
                                w = float(powers[k, m])
                                term = parts[k][i] if w == 1.0 else parts[k][i] * w
                                out = term if out is None else out + term
                            coefs_ref[which, j, 2 * m + i, r, :, at] = out
                return 0

            lax.fori_loop(0, R, body, 0, unroll=2)
    levels = [Rows(ref) for ref in levels]
    for copy in arriving:
        copy.wait()
    load_rows(flat, levels[0])
    for j in range(steps):

        def emit(r, result, j=j):
            for p, v in enumerate(result):
                levels[0].put(p, r, v)
            for b in range(blocks):
                image_ref[j, r, :, b * LANES : (b + 1) * LANES] = product(result[:2], result[2:], b)

        depth_step(levels, coefs_ref.at[1, j], (1, -1), emit)
        levels[0].halo()


def receiver_kernel(fields_ref, coefs_ref, states_ref, flat, flat_sem, *levels):
    arriving = fetch(fields_ref, flat, flat_sem)
    levels = [Rows(ref) for ref in levels]
    steps = coefs_ref.shape[1]
    for copy in arriving:
        copy.wait()
    load_rows(flat, levels[0])
    for which in range(TICKS):
        for j in range(steps):

            def emit(r, result, j=j, which=which):
                for p, v in enumerate(result):
                    levels[0].put(p, r, v)
                    if which == TICKS - 1:
                        for b, w in enumerate(v):
                            states_ref[j, p, r, :, b * LANES : (b + 1) * LANES] = w

            depth_step(levels, coefs_ref.at[which, j], (-1,), emit)
            levels[0].halo()


def source_kernel(
    fields_ref, coefs_ref, receivers_ref, image_ref, owners_ref, slots_ref,
    buffer_ref, state_ref, images, slot_rows, held, sem, slot_sem, flat, flat_sem, *levels
):
    arriving = fetch(fields_ref, flat, flat_sem)
    levels = [Rows(ref) for ref in levels]
    steps = coefs_ref.shape[1]
    blocks = levels[0].blocks
    R = levels[0].R
    for copy in arriving:
        copy.wait()
    load_rows(flat, levels[0])
    for which in range(TICKS):
        for j in range(steps):

            def emit(r, result, j=j, which=which):
                for p, v in enumerate(result):
                    if which == TICKS - 1 and j == steps - 1:
                        for b, w in enumerate(v):
                            state_ref[p, r, :, b * LANES : (b + 1) * LANES] = w
                    else:
                        levels[0].put(p, r, v)
                if which == TICKS - 1:
                    for b in range(blocks):
                        at = slice(b * LANES, (b + 1) * LANES)
                        there = [[receivers_ref[j, p, r, :, at]] for p in (0, 1)]
                        here = [[result[p][b]] for p in (0, 1)]
                        images[j, b, pl.ds(r, SUBS, stride=R), :] = (
                            image_ref[j, r, :, at] + product(here, there, 0)
                        )

            depth_step(levels, coefs_ref.at[which, j], (1,), emit)
            levels[0].halo()
    size = buffer_ref.shape[2]
    peers = buffer_ref.shape[0]
    extra = slot_rows.shape[1]
    tiles_x, tiles_y = images.shape[2] // size, images.shape[1]
    rows = (buffer_ref.shape[1] - extra) // CAP
    for o in range(peers * CAP):
        held[o] = -1
    copies = []
    for p in range(steps * tiles_x * tiles_y):
        j, a, b = p // (tiles_x * tiles_y), p // tiles_y % tiles_x, p % tiles_y
        owner = owners_ref[0, p]
        rank = jnp.int32(0)
        for before in range(p):
            rank = rank + (owners_ref[0, before] == owner).astype(jnp.int32)
        held[owner * CAP + rank] = slots_ref[0, p]
        copies.append(
            pltpu.make_async_copy(
                images.at[j, b, pl.ds(a * rows, rows)],
                buffer_ref.at[owner, pl.ds(pl.multiple_of(rank * rows, rows), rows)],
                sem.at[p],
            )
        )
        copies[-1].start()
    row = lax.broadcasted_iota(jnp.int32, slot_rows.shape[1:], 0)
    for o in range(peers):
        out = jnp.full(slot_rows.shape[1:], -1, jnp.int32)
        for i in range(CAP):
            out = jnp.where(row == i, held[o * CAP + i], out)
        slot_rows[o] = out.astype(jnp.float32)
    last = pltpu.make_async_copy(slot_rows, buffer_ref.at[:, pl.ds(CAP * rows, extra)], slot_sem)
    last.start()
    for copy in copies:
        copy.wait()
    last.wait()


def output_kernel(source_ref, receivers_ref, out_ref, flat, sems):
    R = source_ref.shape[1]
    blocks = flat.shape[2]

    def body(r, _):
        for b in range(blocks):
            at = slice(b * LANES, (b + 1) * LANES)
            for p in (0, 1):
                flat[0, p, b, pl.ds(r, SUBS, stride=R), :] = source_ref[p, r, :, at]
                flat[1, p, b, pl.ds(r, SUBS, stride=R), :] = receivers_ref[receivers_ref.shape[0] - 1, p, r, :, at]
        return 0

    lax.fori_loop(0, R, body, 0, unroll=4)
    copies = [
        pltpu.make_async_copy(flat.at[:, :, b], out_ref.at[:, :, :, pl.ds(b * LANES, LANES)], sems.at[b])
        for b in range(blocks)
    ]
    for copy in copies:
        copy.start()
    for copy in copies:
        copy.wait()


def volume_kernel(received_any, received_ref, out_ref, slots, sem):
    peers, rows, _ = received_ref.shape
    size = out_ref.shape[1]
    copy = pltpu.make_async_copy(received_any.at[:, pl.ds(CAP * size, rows - CAP * size)], slots, sem)
    copy.start()
    out_ref[...] = jnp.zeros_like(out_ref)
    copy.wait()
    for s in range(peers):
        for i in range(CAP):
            slot = slots[s, i, 0].astype(jnp.int32)

            @pl.when(slot >= 0)
            def _(s=s, i=i, slot=slot):
                out_ref[slot] += received_ref[s, i * size : (i + 1) * size, :]


def shifted(shard, axis, by):
    peers = lax.axis_size(axis)
    return lax.ppermute(shard, axis, [(i, i + by) for i in range(peers - by)])


def swapped(shard, axis, bits):
    return lax.ppermute(shard, axis, [(i, i ^ bits) for i in range(lax.axis_size(axis))])


def local(fields, vel_tiles, tile_ids, orders, term_weights, phase_rates, owners, image_slots):
    axis = "depth"
    peers = lax.axis_size(axis)
    cells_x, cells_y = fields.shape[3:]
    size = vel_tiles.shape[1]
    steps, tiles_x, tiles_y = tile_ids.shape[1:]
    terms = phase_rates.shape[0]
    R = cells_x // SUBS
    f32 = jnp.float32

    source_up = shifted(fields[0, 0], axis, 1)
    receiver_up = shifted(fields[0, 1], axis, 1)
    small = shifted(jnp.concatenate([tile_ids.reshape(-1), orders.reshape(-1)])[None], axis, 1)
    ids_up = small[:, : tile_ids.size].reshape(tile_ids.shape)
    orders_up = small[:, tile_ids.size :].reshape(orders.shape)

    far = [(4 * i, swapped(vel_tiles, axis, 4 * i)) for i in range(1, peers // 4)]
    near = [(2, swapped(vel_tiles, axis, 2))]
    near += [(k + 2, swapped(v, axis, 2)) for k, v in far]
    held = [(0, vel_tiles)] + far + near
    half = jnp.stack([v for _, v in held])
    other = swapped(half, axis, 1)
    pieces = [[k for k, _ in held], [k ^ 1 for k, _ in held]]

    blocks = cells_y // LANES
    assert size == LANES and cells_x % SUBS == 0 and cells_y % LANES == 0

    def level(planes):
        return pltpu.VMEM((planes, R + 2, SUBS, cells_y), f32)

    def flat(planes):
        return [pltpu.VMEM((planes, blocks, cells_x, LANES), f32), pltpu.SemaphoreType.DMA((blocks,))]

    coefs, image = pl.pallas_call(
        partial(coefs_kernel, axis, pieces),
        out_shape=(
            jax.ShapeDtypeStruct((TICKS, steps, 2 * terms, R, SUBS, cells_y), f32),
            jax.ShapeDtypeStruct((steps, R, SUBS, cells_y), f32),
        ),
        in_specs=[SMEM] * 6 + [ANY] * 3,
        out_specs=(VMEM, VMEM),
        scratch_shapes=[
            pltpu.VMEM((peers * vel_tiles.shape[0], size, size), f32),
            pltpu.VMEM((blocks, cells_x, LANES), f32),
            pltpu.SemaphoreType.DMA((peers,)),
        ]
        + flat(4)
        + [level(4)] * terms,
        compiler_params=PARAMS,
        name="coefs_and_first_tick",
    )(
        tile_ids, orders, ids_up, orders_up, term_weights, phase_rates, half, other,
        fields.reshape(4, cells_x, cells_y),
    )
    receivers = pl.pallas_call(
        receiver_kernel,
        out_shape=jax.ShapeDtypeStruct((steps, 2, R, SUBS, cells_y), f32),
        in_specs=[ANY, VMEM],
        out_specs=VMEM,
        scratch_shapes=flat(2) + [level(2)] * terms,
        compiler_params=PARAMS,
        name="receiver_ticks",
    )(receiver_up, coefs)
    extra = SUBS
    buffer, source = pl.pallas_call(
        source_kernel,
        out_shape=(
            jax.ShapeDtypeStruct((peers, CAP * size + extra, size), f32),
            jax.ShapeDtypeStruct((2, R, SUBS, cells_y), f32),
        ),
        in_specs=[ANY] + [VMEM] * 3 + [SMEM] * 2,
        out_specs=(ANY, VMEM),
        scratch_shapes=[
            pltpu.VMEM((steps, blocks, cells_x, LANES), f32),
            pltpu.VMEM((peers, extra, size), f32),
            pltpu.SMEM((peers * CAP,), jnp.int32),
            pltpu.SemaphoreType.DMA((steps * tiles_x * tiles_y,)),
            pltpu.SemaphoreType.DMA,
        ]
        + flat(2)
        + [level(2)] * terms,
        compiler_params=PARAMS,
        name="source_ticks_and_seats",
    )(source_up, coefs, receivers, image, owners, image_slots)
    received = lax.all_to_all(buffer, axis, split_axis=0, concat_axis=0, tiled=True)
    wavefields = pl.pallas_call(
        output_kernel,
        out_shape=jax.ShapeDtypeStruct((2, 2, cells_x, cells_y), f32),
        in_specs=[VMEM, VMEM],
        out_specs=ANY,
        scratch_shapes=[pltpu.VMEM((2, 2, blocks, cells_x, LANES), f32), pltpu.SemaphoreType.DMA((blocks,))],
        compiler_params=PARAMS,
        name="wavefields",
    )(source, receivers)
    volume = pl.pallas_call(
        volume_kernel,
        out_shape=jax.ShapeDtypeStruct((IMG_SLOTS, size, size), f32),
        in_specs=[ANY, VMEM],
        out_specs=VMEM,
        scratch_shapes=[pltpu.SMEM((peers, extra, size), f32), pltpu.SemaphoreType.DMA],
        compiler_params=PARAMS,
        name="image_volume",
    )(received, received)
    return volume, wavefields[None]


def solution(mesh):
    placed = (
        P(("groups", "depth"), None, None, None, None),
        P(("groups", "depth"), None, None),
        P(("groups", "depth"), None, None, None),
        P(("groups", "depth"), None),
        P(),
        P(),
        P(("groups", "depth"), None),
        P(("groups", "depth"), None),
    )
    return jax.shard_map(
        local,
        mesh=mesh,
        in_specs=placed,
        out_specs=(
            P(("groups", "depth"), None, None),
            P(("groups", "depth"), None, None, None, None),
        ),
        check_vma=False,
    )
```

```python
from functools import partial

import jax
import jax.numpy as jnp
import numpy as np
from jax import lax
from jax.experimental import pallas as pl
from jax.experimental.pallas import tpu as pltpu
from jax.sharding import PartitionSpec as P

TICKS = 2
CAP = 2
IMG_SLOTS = 8
LANES = 128
SUBS = 8
VMEM = pl.BlockSpec(memory_space=pltpu.VMEM)
SMEM = pl.BlockSpec(memory_space=pltpu.SMEM)
ANY = pl.BlockSpec(memory_space=pl.ANY)
PARAMS = pltpu.CompilerParams(vmem_limit_bytes=18 * 2**20)


def in_vmem(x):
    return pltpu.with_memory_space_constraint(x, pltpu.VMEM)


def in_powers(terms):
    rows = np.zeros((terms, terms))
    polys = [np.array([1.0]), np.array([-1.0, 1.0])]
    while len(polys) < terms:
        grown = np.convolve(polys[-1], [-2.0, 2.0])
        grown[: len(polys[-2])] -= polys[-2]
        polys.append(grown)
    for k in range(terms):
        rows[k, : len(polys[k])] = polys[k] / 8.0 ** np.arange(len(polys[k]))
    return rows


def fitted():
    nodes = 0.25 * (1.0 - np.cos((np.arange(400) + 0.5) * np.pi / 400)) / 2.0
    r = np.sqrt(nodes)
    sine = np.polynomial.chebyshev.Chebyshev.fit(nodes, np.sqrt(2.0) * np.sin(np.pi * r) / r, 4)
    cosine = np.polynomial.chebyshev.Chebyshev.fit(nodes, np.sqrt(2.0) * np.cos(np.pi * r), 4)
    make = np.polynomial.polynomial.Polynomial
    return (
        [float(c) for c in sine.convert(kind=make).coef],
        [float(c) for c in cosine.convert(kind=make).coef],
    )


SINE, COSINE = fitted()


def horner(x, coefs):
    out = coefs[-1] * x + coefs[-2]
    for c in coefs[-3::-1]:
        out = out * x + c
    return out


def cos_sin(turns):
    r = turns - jnp.round(turns)
    r2 = r * r
    s = r * horner(r2, SINE)
    c = horner(r2, COSINE)
    return 1.0 - s * s, s * c


def lane_sums(cells_y, terms):
    one = 2 * np.eye(cells_y) + np.eye(cells_y, k=1) + np.eye(cells_y, k=-1)
    side = np.concatenate([np.linalg.matrix_power(one, k) for k in range(1, terms)], 1)
    return jnp.asarray(np.concatenate([side, side], 0), jnp.bfloat16)


class Rows:
    def __init__(self, ref, edge, first=0, planes=None):
        self.ref, self.edge, self.first = ref, edge, first
        self.planes = ref.shape[0] if planes is None else planes
        self.R = ref.shape[1] - 2 * edge
        self.blocks = ref.shape[3] // LANES

    def get(self, p, r, b):
        return self.ref[self.first + p, r + self.edge, :, b * LANES : (b + 1) * LANES]

    def put(self, p, r, b, value):
        self.ref[self.first + p, r + self.edge, :, b * LANES : (b + 1) * LANES] = value

    def halo(self):
        sub = lax.broadcasted_iota(jnp.int32, (SUBS, LANES), 0)
        R = self.R
        for p in range(self.planes):
            for b in range(self.blocks):
                for h in range(1, self.edge + 1):
                    low = 0.0 if h == 1 else -self.get(p, h - 2, b)
                    self.put(p, -h, b, jnp.where(sub == 0, low, pltpu.roll(self.get(p, R - h, b), 1, 0)))
                    high = 0.0 if h == 1 else -self.get(p, R + 1 - h, b)
                    turned = pltpu.roll(self.get(p, h - 1, b), SUBS - 1, 0)
                    self.put(p, R - 1 + h, b, jnp.where(sub == SUBS - 1, high, turned))


def along_y(state, sides_ref, sums):
    rows, cells_y = state.ref.shape[1], state.ref.shape[3]
    side = sides_ref[...]
    for p in range(state.planes):
        here = state.ref[state.first + p].reshape(rows * SUBS, cells_y)
        high = here.astype(jnp.bfloat16)
        low = (here - high.astype(jnp.float32)).astype(jnp.bfloat16)
        out = jnp.dot(jnp.concatenate([high, low], 1), side, preferred_element_type=jnp.float32)
        for k in range(sums.shape[0]):
            sums[k, p] = out[:, k * cells_y : (k + 1) * cells_y].reshape(rows, SUBS, cells_y)


def chained(carry, value, length):
    kept = []
    for c in carry:
        kept.append(value)
        value = value + c
    if len(carry) < length:
        kept.append(value)
    return kept, value


def depth_step(state, sums, coefs, sign, emit, unroll=8):
    terms, edge = sums.shape[0] + 1, state.edge
    for b in range(state.blocks):
        at = slice(b * LANES, (b + 1) * LANES)

        def body(r, carry):
            kept, total = [], [None, None]
            for k in range(terms):
                if k == 0:
                    re, im = state.get(0, r, b), state.get(1, r, b)
                else:
                    both = []
                    for p in (0, 1):
                        new, value = chained(
                            carry[2 * (k - 1) + p], sums[k - 1, p, r + edge + k, :, at], 2 * k
                        )
                        kept.append(new)
                        both.append(value)
                    re, im = both
                a, s = coefs[2 * k, r, :, at], coefs[2 * k + 1, r, :, at]
                x, y, u, v = a * re, a * im, s * im, s * re
                x, y = (x - u, y + v) if sign > 0 else (x + u, y - v)
                total = [x, y] if k == 0 else [total[0] + x, total[1] + y]
            emit(r, b, *total)
            return kept

        start = []
        for k in range(1, terms):
            for p in (0, 1):
                chain = []
                for r in range(-k, k):
                    chain, _ = chained(chain, sums[k - 1, p, r + edge, :, at], 2 * k)
                start.append(chain)
        lax.fori_loop(0, state.R, body, start, unroll=unroll)


def fetch(field_ref, flat, sem):
    copies = [
        pltpu.make_async_copy(field_ref.at[:, :, pl.ds(b * LANES, LANES)], flat.at[:, b], sem.at[b])
        for b in range(flat.shape[1])
    ]
    for copy in copies:
        copy.start()
    return copies


def load_rows(flat, state):
    def body(r, _):
        for p in range(state.planes):
            for b in range(state.blocks):
                state.put(p, r, b, flat[state.first + p, b, pl.ds(r, SUBS, stride=state.R), :])
        return 0

    lax.fori_loop(0, state.R, body, 0, unroll=4)
    state.halo()


def stack_kernel(*refs):
    parts, (ext, out, rows, sems) = refs[:-4], refs[-4:]
    edge = (ext.shape[1] - rows.shape[1]) // 2
    copies = [pltpu.make_async_copy(part, out.at[i], sems.at[i]) for i, part in enumerate(parts)]
    copies.append(
        pltpu.make_async_copy(
            ext.at[pl.ds(2, 2), pl.ds(edge, rows.shape[1])], rows, sems.at[len(parts)]
        )
    )
    for copy in copies:
        copy.start()
    for copy in copies:
        copy.wait()


def along_kernel(fields_ref, sides_ref, ids_ref, orders_ref, ext, sums, flat, flat_sem):
    for copy in fetch(fields_ref, flat, flat_sem):
        copy.wait()
    edge = sums.shape[1]
    load_rows(flat, Rows(ext, edge))
    for pair in (0, 1):
        along_y(Rows(ext, edge, 2 * pair, 2), sides_ref, sums.at[pair])


def series(slow, orders_ref, weights_ref, rates_ref, coefs_ref, j):
    terms = rates_ref.shape[0]
    powers = in_powers(terms)
    R = coefs_ref.shape[2]
    total = weights_ref[0]
    for k in range(1, terms - 1):
        total = total + weights_ref[k]
    base = [1.0 - total] + [weights_ref[k] for k in range(terms - 1)]
    turn = [rates_ref[k] * (0.5 / np.pi) for k in range(terms)]
    scale = [jnp.where(k <= orders_ref[0, j], base[k], 0.0) for k in range(terms)]

    def body(r, _):
        for b in range(slow.shape[0]):
            at = slice(b * LANES, (b + 1) * LANES)
            here = slow[b, pl.ds(r, SUBS, stride=R), :]
            parts = []
            for k in range(terms):
                c, s = cos_sin(here * turn[k])
                parts.append((c * scale[k], s * scale[k]))
            for m in range(terms):
                for i in (0, 1):
                    out = None
                    for k in range(m, terms):
                        w = float(powers[k, m])
                        term = parts[k][i] if abs(w) == 1.0 else parts[k][i] * abs(w)
                        if out is None:
                            out = term if w > 0 else -term
                        else:
                            out = out + term if w > 0 else out - term
                    coefs_ref[j, 2 * m + i, r, :, at] = out
        return 0

    lax.fori_loop(0, R, body, 0, unroll=4)


def first_source_kernel(
    axis, pieces, ids_ref, orders_ref, ids_up_ref, weights_ref, rates_ref, sides_ref, ext_in, sums_in, *rest
):
    tiles, (coefs_ref, states_ref, out_ref, slow_up), (library, slow, sems, out_sem, ext, sums) = (
        rest[: len(pieces)],
        rest[len(pieces) : len(pieces) + 4],
        rest[len(pieces) + 4 :],
    )
    per = library.shape[0] // sum(len(at) for at in pieces)
    copies = []
    for ref, at in zip(tiles, pieces):
        for i, k in enumerate(at):
            copies.append(
                pltpu.make_async_copy(ref.at[i], library.at[pl.ds(k * per, per)], sems.at[len(copies)])
            )
            copies[-1].start()
    for copy in copies:
        copy.wait()
    me = lax.axis_index(axis)
    steps, tiles_x, tiles_y = ids_ref.shape[-3:]
    size = library.shape[1]
    for j in range(steps):
        for a in range(tiles_x):
            for b in range(tiles_y):
                for ids, to in ((ids_ref, slow), (ids_up_ref, slow_up.at[j])):
                    tile = ids[0, j, a, b]
                    to[b, a * size : (a + 1) * size, :] = library[(tile // per ^ me) * per + tile % per]
        series(slow, orders_ref, weights_ref, rates_ref, coefs_ref, j)
        edge = sums.shape[0]
        state = Rows(ext_in if j == 0 else ext, edge, 0, 2)
        into = Rows(ext, edge)
        if j:
            state.halo()
            along_y(state, sides_ref, sums)

        def emit(r, b, re, im, j=j, into=into):
            for p, value in enumerate((re, im)):
                states_ref[j, p, r, :, b * LANES : (b + 1) * LANES] = value
                if j + 1 < steps:
                    into.put(p, r, b, value)

        depth_step(state, sums if j else sums_in.at[0], coefs_ref.at[j], 1, emit)
    copy = pltpu.make_async_copy(states_ref.at[steps - 1], out_ref, out_sem)
    copy.start()
    copy.wait()


def first_image_kernel(
    orders_up_ref, weights_ref, rates_ref, slow_up, sides_ref, ext_in, sums_in, coefs_ref, states_ref,
    coefs_up_ref, image_ref, ext, sums
):
    steps = coefs_ref.shape[0]
    edge = sums.shape[0]
    into = Rows(ext, edge)
    for j in range(steps):
        series(slow_up.at[j], orders_up_ref, weights_ref, rates_ref, coefs_up_ref, j)
        state = into if j else Rows(ext_in, edge, 2, 2)
        if j:
            state.halo()
            along_y(state, sides_ref, sums)

        def emit(r, b, re, im, j=j):
            at = slice(b * LANES, (b + 1) * LANES)
            image_ref[j, r, :, at] = re * states_ref[j, 0, r, :, at] + im * states_ref[j, 1, r, :, at]
            if j + 1 < steps:
                into.put(0, r, b, re)
                into.put(1, r, b, im)

        depth_step(state, sums if j else sums_in.at[1], coefs_ref.at[j], -1, emit)


def take_rows(rows_ref, state, sem):
    copy = pltpu.make_async_copy(rows_ref, state.ref.at[:, pl.ds(state.edge, state.R)], sem)
    copy.start()
    copy.wait()
    state.halo()


def receiver_kernel(rows_ref, coefs_up_ref, coefs_ref, sides_ref, states_ref, sem, ext, sums):
    steps = coefs_ref.shape[0]
    state = Rows(ext, sums.shape[0])
    take_rows(rows_ref, state, sem)
    for which, coefs in enumerate((coefs_up_ref, coefs_ref)):
        for j in range(steps):
            final = which == 1 and j == steps - 1

            def emit(r, b, re, im, j=j, which=which, final=final):
                for p, value in enumerate((re, im)):
                    if not final:
                        state.put(p, r, b, value)
                    if which == 1:
                        states_ref[j, p, r, :, b * LANES : (b + 1) * LANES] = value

            along_y(state, sides_ref, sums)
            depth_step(state, sums, coefs.at[j], -1, emit)
            if not final:
                state.halo()


def source_kernel(
    rows_ref, coefs_ref, sides_ref, receivers_ref, image_ref, owners_ref, slots_ref,
    buffer_ref, state_ref, images, slot_rows, held, sem, slot_sem, ext, sums
):
    steps = coefs_ref.shape[0]
    state = Rows(ext, sums.shape[0])
    R = state.R
    take_rows(rows_ref, state, slot_sem)
    for j in range(steps):
        final = j == steps - 1

        def emit(r, b, re, im, j=j, final=final):
            at = slice(b * LANES, (b + 1) * LANES)
            for p, value in enumerate((re, im)):
                if final:
                    state_ref[p, r, :, at] = value
                else:
                    state.put(p, r, b, value)
            images[j, b, pl.ds(r, SUBS, stride=R), :] = (
                image_ref[j, r, :, at]
                + re * receivers_ref[j, 0, r, :, at]
                + im * receivers_ref[j, 1, r, :, at]
            )

        along_y(state, sides_ref, sums)
        depth_step(state, sums, coefs_ref.at[j], 1, emit)
        if not final:
            state.halo()
    size = buffer_ref.shape[2]
    peers = buffer_ref.shape[0]
    extra = slot_rows.shape[1]
    tiles_x, tiles_y = images.shape[2] // size, images.shape[1]
    rows = (buffer_ref.shape[1] - extra) // CAP
    for o in range(peers * CAP):
        held[o] = -1
    copies = []
    for p in range(steps * tiles_x * tiles_y):
        j, a, b = p // (tiles_x * tiles_y), p // tiles_y % tiles_x, p % tiles_y
        owner = owners_ref[0, p]
        rank = jnp.int32(0)
        for before in range(p):
            rank = rank + (owners_ref[0, before] == owner).astype(jnp.int32)
        held[owner * CAP + rank] = slots_ref[0, p]
        copies.append(
            pltpu.make_async_copy(
                images.at[j, b, pl.ds(a * rows, rows)],
                buffer_ref.at[owner, pl.ds(pl.multiple_of(rank * rows, rows), rows)],
                sem.at[p],
            )
        )
        copies[-1].start()
    lane = lax.broadcasted_iota(jnp.int32, slot_rows.shape[1:], 1)
    for o in range(peers):
        out = jnp.full(slot_rows.shape[1:], -1, jnp.int32)
        for i in range(CAP):
            out = jnp.where(lane == i, held[o * CAP + i], out)
        slot_rows[o] = out.astype(jnp.float32)
    last = pltpu.make_async_copy(slot_rows, buffer_ref.at[:, pl.ds(CAP * rows, extra)], slot_sem)
    last.start()
    for copy in copies:
        copy.wait()
    last.wait()


def output_kernel(source_ref, receivers_ref, out_ref, flat, sems):
    R = source_ref.shape[1]
    blocks = flat.shape[2]

    def body(r, _):
        for b in range(blocks):
            at = slice(b * LANES, (b + 1) * LANES)
            for p in (0, 1):
                flat[0, p, b, pl.ds(r, SUBS, stride=R), :] = source_ref[p, r, :, at]
                flat[1, p, b, pl.ds(r, SUBS, stride=R), :] = receivers_ref[receivers_ref.shape[0] - 1, p, r, :, at]
        return 0

    lax.fori_loop(0, R, body, 0, unroll=4)
    copies = [
        pltpu.make_async_copy(flat.at[:, :, b], out_ref.at[:, :, :, pl.ds(b * LANES, LANES)], sems.at[b])
        for b in range(blocks)
    ]
    for copy in copies:
        copy.start()
    for copy in copies:
        copy.wait()


def volume_kernel(received_ref, out_ref, slots, sem):
    peers, rows, _ = received_ref.shape
    size = out_ref.shape[1]
    copy = pltpu.make_async_copy(received_ref.at[:, pl.ds(CAP * size, 1)], slots, sem)
    copy.start()
    out_ref[...] = jnp.zeros_like(out_ref)
    copy.wait()
    for s in range(peers):
        for i in range(CAP):
            slot = slots[s, 0, i].astype(jnp.int32)

            @pl.when(slot >= 0)
            def _(s=s, i=i, slot=slot):
                out_ref[slot] += received_ref[s, i * size : (i + 1) * size, :]


def shifted(shard, axis, by):
    peers = lax.axis_size(axis)
    return lax.ppermute(shard, axis, [(i, i + by) for i in range(peers - by)])


def swapped(shard, axis, bits):
    return lax.ppermute(shard, axis, [(i, i ^ bits) for i in range(lax.axis_size(axis))])


def local(fields, vel_tiles, tile_ids, orders, term_weights, phase_rates, owners, image_slots):
    axis = "depth"
    peers = lax.axis_size(axis)
    cells_x, cells_y = fields.shape[3:]
    size = vel_tiles.shape[1]
    steps, tiles_x, tiles_y = tile_ids.shape[1:]
    terms = phase_rates.shape[0]
    R = cells_x // SUBS
    f32 = jnp.float32

    ids_up = shifted(tile_ids, axis, 1)
    orders_up = shifted(orders, axis, 1)
    far = [(4 * i, swapped(vel_tiles, axis, 4 * i)) for i in range(1, peers // 4)]
    beside = [(2, swapped(vel_tiles, axis, 2))]
    beside += [(k + 2, swapped(v, axis, 2)) for k, v in far]
    held = [(0, vel_tiles)] + far + beside
    blocks = cells_y // LANES
    assert size == LANES and cells_x % SUBS == 0 and cells_y % LANES == 0

    edge = terms - 1
    sides = lane_sums(cells_y, terms)

    def flat(planes):
        return [pltpu.VMEM((planes, blocks, cells_x, LANES), f32), pltpu.SemaphoreType.DMA((blocks,))]

    def work(planes):
        return [
            pltpu.VMEM((planes, R + 2 * edge, SUBS, cells_y), f32),
            pltpu.VMEM((edge, 2, R + 2 * edge, SUBS, cells_y), f32),
        ]

    planes = (R, SUBS, cells_y)
    padded = (R + 2 * edge, SUBS, cells_y)
    call = partial(pl.pallas_call, compiler_params=PARAMS)
    ext, sums = call(
        along_kernel,
        out_shape=(pltpu.VMEM((4,) + padded, f32), pltpu.VMEM((2, edge, 2) + padded, f32)),
        in_specs=[ANY, VMEM, SMEM, SMEM],
        out_specs=(VMEM, VMEM),
        scratch_shapes=flat(4),
        cost_estimate=pl.CostEstimate(flops=2**32, bytes_accessed=2**23, transcendentals=0),
        name="along_y",
    )(fields.reshape(4, cells_x, cells_y), sides, ids_up, orders_up)
    ext, sums = in_vmem(ext), in_vmem(sums)
    half, rows = call(
        stack_kernel,
        out_shape=(
            pltpu.VMEM((len(held),) + vel_tiles.shape, f32),
            pltpu.VMEM((2,) + planes, f32),
        ),
        in_specs=[ANY] * len(held) + [VMEM],
        out_specs=(VMEM, VMEM),
        scratch_shapes=[pltpu.SemaphoreType.DMA((len(held) + 1,))],
        name="stack_tiles",
    )(*[v for _, v in held], ext)
    other = swapped(half, axis, 1)
    pieces = [[k for k, _ in held], [k ^ 1 for k, _ in held]]
    receiver_up = shifted(rows, axis, 1)
    coefs, states, sent, slow_up = call(
        partial(first_source_kernel, axis, pieces),
        out_shape=(
            pltpu.VMEM((steps, 2 * terms) + planes, f32),
            pltpu.VMEM((steps, 2) + planes, f32),
            pltpu.HBM((2,) + planes, f32),
            pltpu.VMEM((steps, blocks, cells_x, LANES), f32),
        ),
        in_specs=[SMEM] * 5 + [VMEM] * 3 + [ANY] * 2,
        out_specs=(VMEM, VMEM, ANY, VMEM),
        scratch_shapes=[
            pltpu.VMEM((peers * vel_tiles.shape[0], size, size), f32),
            pltpu.VMEM((blocks, cells_x, LANES), f32),
            pltpu.SemaphoreType.DMA((peers,)),
            pltpu.SemaphoreType.DMA,
        ]
        + work(2),
        name="first_sources",
    )(tile_ids, orders, ids_up, term_weights, phase_rates, sides, ext, sums, half, other)
    source_up = shifted(sent, axis, 1)
    coefs, states, slow_up = in_vmem(coefs), in_vmem(states), in_vmem(slow_up)
    coefs_up, image = call(
        first_image_kernel,
        out_shape=(
            pltpu.VMEM((steps, 2 * terms) + planes, f32),
            pltpu.VMEM((steps,) + planes, f32),
        ),
        in_specs=[SMEM] * 3 + [VMEM] * 6,
        out_specs=(VMEM, VMEM),
        scratch_shapes=work(2),
        name="first_images",
    )(orders_up, term_weights, phase_rates, slow_up, sides, ext, sums, coefs, states)
    receivers = in_vmem(
        call(
            receiver_kernel,
            out_shape=pltpu.VMEM((steps, 2) + planes, f32),
            in_specs=[ANY] + [VMEM] * 3,
            out_specs=VMEM,
            scratch_shapes=[pltpu.SemaphoreType.DMA] + work(2),
            name="receiver_ticks",
        )(receiver_up, in_vmem(coefs_up), coefs, sides)
    )
    extra = SUBS
    buffer, source = call(
        source_kernel,
        out_shape=(
            pltpu.HBM((peers, CAP * size + extra, size), f32),
            pltpu.HBM((2,) + planes, f32),
        ),
        in_specs=[ANY] + [VMEM] * 4 + [SMEM] * 2,
        out_specs=(ANY, VMEM),
        scratch_shapes=[
            pltpu.VMEM((steps, blocks, cells_x, LANES), f32),
            pltpu.VMEM((peers, extra, size), f32),
            pltpu.SMEM((peers * CAP,), jnp.int32),
            pltpu.SemaphoreType.DMA((steps * tiles_x * tiles_y,)),
            pltpu.SemaphoreType.DMA,
        ]
        + work(2),
        name="source_tick_and_seats",
    )(source_up, coefs, sides, receivers, in_vmem(image), owners, image_slots)
    received = lax.all_to_all(buffer, axis, split_axis=0, concat_axis=0, tiled=True)
    wavefields = pl.pallas_call(
        output_kernel,
        out_shape=jax.ShapeDtypeStruct((2, 2, cells_x, cells_y), f32),
        in_specs=[VMEM, VMEM],
        out_specs=ANY,
        scratch_shapes=[
            pltpu.VMEM((2, 2, blocks, cells_x, LANES), f32),
            pltpu.SemaphoreType.DMA((blocks,)),
        ],
        compiler_params=PARAMS,
        name="wavefields",
    )(source, receivers)
    volume = pl.pallas_call(
        volume_kernel,
        out_shape=jax.ShapeDtypeStruct((IMG_SLOTS, size, size), f32),
        in_specs=[VMEM],
        out_specs=VMEM,
        scratch_shapes=[pltpu.SMEM((peers, 1, size), f32), pltpu.SemaphoreType.DMA],
        compiler_params=PARAMS,
        name="image_volume",
    )(in_vmem(received))
    return volume, wavefields[None]


def solution(mesh):
    placed = (
        P(("groups", "depth"), None, None, None, None),
        P(("groups", "depth"), None, None),
        P(("groups", "depth"), None, None, None),
        P(("groups", "depth"), None),
        P(),
        P(),
        P(("groups", "depth"), None),
        P(("groups", "depth"), None),
    )
    return jax.shard_map(
        local,
        mesh=mesh,
        in_specs=placed,
        out_specs=(
            P(("groups", "depth"), None, None),
            P(("groups", "depth"), None, None, None, None),
        ),
        check_vma=False,
    )
```

```python
from functools import partial

import jax
import jax.numpy as jnp
import numpy as np
from jax import lax
from jax.experimental import pallas as pl
from jax.experimental.pallas import tpu as pltpu
from jax.sharding import PartitionSpec as P

TICKS = 2
CAP = 2
IMG_SLOTS = 8
LANES = 128
SUBS = 8
VMEM = pl.BlockSpec(memory_space=pltpu.VMEM)
SMEM = pl.BlockSpec(memory_space=pltpu.SMEM)
ANY = pl.BlockSpec(memory_space=pl.ANY)
PARAMS = pltpu.CompilerParams(vmem_limit_bytes=14 * 2**20)


def in_vmem(x):
    return pltpu.with_memory_space_constraint(x, pltpu.VMEM)


def in_hbm(x):
    return pltpu.with_memory_space_constraint(x, pltpu.HBM)


def in_powers(terms):
    rows = np.zeros((terms, terms))
    polys = [np.array([1.0]), np.array([-1.0, 1.0])]
    while len(polys) < terms:
        grown = np.convolve(polys[-1], [-2.0, 2.0])
        grown[: len(polys[-2])] -= polys[-2]
        polys.append(grown)
    for k in range(terms):
        rows[k, : len(polys[k])] = polys[k] / 8.0 ** np.arange(len(polys[k]))
    lead = np.diag(rows).copy()
    return rows / lead, lead


def fitted():
    nodes = 0.25 * (1.0 - np.cos((np.arange(400) + 0.5) * np.pi / 400)) / 2.0
    r = np.sqrt(nodes)
    sine = np.polynomial.chebyshev.Chebyshev.fit(nodes, np.sqrt(2.0) * np.sin(np.pi * r) / r, 4)
    cosine = np.polynomial.chebyshev.Chebyshev.fit(nodes, np.sqrt(2.0) * np.cos(np.pi * r), 4)
    make = np.polynomial.polynomial.Polynomial
    return (
        [float(c) for c in sine.convert(kind=make).coef],
        [float(c) for c in cosine.convert(kind=make).coef],
    )


SINE, COSINE = fitted()
ROUNDER = 1.5 * 2.0**23


def horner(x, coefs):
    out = coefs[-1] * x + coefs[-2]
    for c in coefs[-3::-1]:
        out = out * x + c
    return out


def cos_sin(turns):
    r = turns - ((turns + ROUNDER) - ROUNDER)
    r2 = r * r
    s = r * horner(r2, SINE)
    c = horner(r2, COSINE)
    return 1.0 - s * s, s * c


def lane_sums(cells_y, terms):
    one = 2 * np.eye(cells_y) + np.eye(cells_y, k=1) + np.eye(cells_y, k=-1)
    _, lead = in_powers(terms)
    side = np.concatenate([lead[k] * np.linalg.matrix_power(one, k) for k in range(1, terms)], 1)
    return jnp.asarray(np.concatenate([side, side], 0), jnp.bfloat16)


class Rows:
    def __init__(self, ref, edge, first=0, planes=None):
        self.ref, self.edge, self.first = ref, edge, first
        self.planes = ref.shape[0] if planes is None else planes
        self.R = ref.shape[1] - 2 * edge
        self.blocks = ref.shape[3] // LANES

    def get(self, p, r, b):
        return self.ref[self.first + p, r + self.edge, :, b * LANES : (b + 1) * LANES]

    def put(self, p, r, b, value):
        self.ref[self.first + p, r + self.edge, :, b * LANES : (b + 1) * LANES] = value

    def halo(self):
        sub = lax.broadcasted_iota(jnp.int32, (SUBS, LANES), 0)
        R = self.R
        for p in range(self.planes):
            for b in range(self.blocks):
                for h in range(1, self.edge + 1):
                    low = 0.0 if h == 1 else -self.get(p, h - 2, b)
                    self.put(p, -h, b, jnp.where(sub == 0, low, pltpu.roll(self.get(p, R - h, b), 1, 0)))
                    high = 0.0 if h == 1 else -self.get(p, R + 1 - h, b)
                    turned = pltpu.roll(self.get(p, h - 1, b), SUBS - 1, 0)
                    self.put(p, R - 1 + h, b, jnp.where(sub == SUBS - 1, high, turned))


def along_y(state, sides_ref, sums):
    rows, cells_y = state.ref.shape[1], state.ref.shape[3]
    side = sides_ref[...]
    for p in range(state.planes):
        here = state.ref[state.first + p].reshape(rows * SUBS, cells_y)
        high = here.astype(jnp.bfloat16)
        low = (here - high.astype(jnp.float32)).astype(jnp.bfloat16)
        out = jnp.dot(jnp.concatenate([high, low], 1), side, preferred_element_type=jnp.float32)
        for k in range(sums.shape[0]):
            sums[k, p] = out[:, k * cells_y : (k + 1) * cells_y].reshape(rows, SUBS, cells_y)


def chained(carry, value, length):
    kept = []
    for c in carry:
        kept.append(value)
        value = value + c
    if len(carry) < length:
        kept.append(value)
    return kept, value


def depth_step(state, sums, coefs, sign, emit, unroll=8):
    terms, edge = sums.shape[0] + 1, state.edge
    for b in range(state.blocks):
        at = slice(b * LANES, (b + 1) * LANES)

        def body(r, carry):
            kept, total = [], [None, None]
            for k in range(terms):
                if k == 0:
                    re, im = state.get(0, r, b), state.get(1, r, b)
                else:
                    both = []
                    for p in (0, 1):
                        new, value = chained(
                            carry[2 * (k - 1) + p], sums[k - 1, p, r + edge + k, :, at], 2 * k
                        )
                        kept.append(new)
                        both.append(value)
                    re, im = both
                a, s = coefs[2 * k, r, :, at], coefs[2 * k + 1, r, :, at]
                x, y, u, v = a * re, a * im, s * im, s * re
                x, y = (x - u, y + v) if sign > 0 else (x + u, y - v)
                total = [x, y] if k == 0 else [total[0] + x, total[1] + y]
            emit(r, b, *total)
            return kept

        start = []
        for k in range(1, terms):
            for p in (0, 1):
                chain = []
                for r in range(-k, k):
                    chain, _ = chained(chain, sums[k - 1, p, r + edge, :, at], 2 * k)
                start.append(chain)
        lax.fori_loop(0, state.R, body, start, unroll=unroll)


def fetch(field_ref, flat, sem):
    copies = [
        pltpu.make_async_copy(field_ref.at[:, :, pl.ds(b * LANES, LANES)], flat.at[:, b], sem.at[b])
        for b in range(flat.shape[1])
    ]
    for copy in copies:
        copy.start()
    return copies


def load_rows(flat, state):
    def body(r, _):
        for p in range(state.planes):
            for b in range(state.blocks):
                state.put(p, r, b, flat[state.first + p, b, pl.ds(r, SUBS, stride=state.R), :])
        return 0

    lax.fori_loop(0, state.R, body, 0, unroll=4)
    state.halo()


def stack_kernel(*refs):
    parts, (out, sems) = refs[:-2], refs[-2:]
    copies = [pltpu.make_async_copy(part, out.at[i], sems.at[i]) for i, part in enumerate(parts)]
    for copy in copies:
        copy.start()
    for copy in copies:
        copy.wait()


def words_of(ids_ref, orders_ref):
    _, steps, tiles_x, tiles_y = ids_ref.shape
    for j in range(steps):
        yield orders_ref[0, j]
        for a in range(tiles_x):
            for b in range(tiles_y):
                yield ids_ref[0, j, a, b]


def place_tiles(axis, tiles, tile_of, slow):
    _, per, size, _ = tiles[0].shape
    me = lax.axis_index(axis)
    for a in range(slow.shape[1] // size):
        for b in range(slow.shape[0]):
            tile = tile_of(a, b)
            apart = tile // per ^ me
            for low, ref in enumerate(tiles):

                @pl.when((apart & 3) == low)
                def _(a=a, b=b, ref=ref, group=apart >> 2, tile=tile):
                    slow[b, a * size : (a + 1) * size, :] = ref[group, tile % per]


def rows_kernel(
    ids_ref, orders_ref, fields_ref, sides_ref, ext, rows, source_sums, receiver_sums, flat, flat_sem, sem
):
    arriving = fetch(fields_ref, flat, flat_sem)
    R = rows.shape[1] - 1
    edge = (ext.shape[1] - R) // 2
    lane = lax.broadcasted_iota(jnp.int32, rows.shape[2:], 1)
    words = jnp.zeros(rows.shape[2:], jnp.int32)
    for i, word in enumerate(words_of(ids_ref, orders_ref)):
        words = jnp.where(lane == i, word, words)
    for p in range(rows.shape[0]):
        rows[p, R] = words.astype(jnp.float32)
    for copy in arriving:
        copy.wait()
    load_rows(flat, Rows(ext, edge))
    copy = pltpu.make_async_copy(
        ext.at[pl.ds(2, 2), pl.ds(edge, R)], rows.at[:, pl.ds(0, R)], sem
    )
    copy.start()
    along_y(Rows(ext, edge, 0, 2), sides_ref, source_sums)
    along_y(Rows(ext, edge, 2, 2), sides_ref, receiver_sums)
    copy.wait()


def series(slow, order, weights_ref, rates_ref, coefs_ref, j):
    terms = rates_ref.shape[0]
    powers, _ = in_powers(terms)
    R = coefs_ref.shape[2]
    total = weights_ref[0]
    for k in range(1, terms - 1):
        total = total + weights_ref[k]
    base = [1.0 - total] + [weights_ref[k] for k in range(terms - 1)]
    turn = [rates_ref[k] * (0.5 / np.pi) for k in range(terms)]
    scale = [jnp.where(k <= order, base[k], 0.0) for k in range(terms)]

    def row(r, _):
        for b in range(slow.shape[0]):
            at = slice(b * LANES, (b + 1) * LANES)
            here = slow[b, pl.ds(r, SUBS, stride=R), :]
            parts = []
            for k in range(terms):
                c, s = cos_sin(here * turn[k])
                parts.append((c * scale[k], s * scale[k]))
            for m in range(terms):
                for i in (0, 1):
                    out = None
                    for k in range(m, terms):
                        w = float(powers[k, m])
                        term = parts[k][i] if abs(w) == 1.0 else parts[k][i] * abs(w)
                        if out is None:
                            out = term if w > 0 else -term
                        else:
                            out = out + term if w > 0 else out - term
                    coefs_ref[j, 2 * m + i, r, :, at] = out
        return 0

    lax.fori_loop(0, R, row, 0, unroll=8)


def first_source_kernel(
    axis, ids_ref, orders_ref, weights_ref, rates_ref, sides_ref, ext_in, sums_in, t0, t1, t2, t3,
    coefs_ref, states_ref, sent_ref, slow, ext, sums
):
    steps = ids_ref.shape[1]
    for j in range(steps):
        place_tiles(axis, (t0, t1, t2, t3), lambda a, b, j=j: ids_ref[0, j, a, b], slow)
        edge = sums.shape[0]
        state = Rows(ext_in if j == 0 else ext, edge, 0, 2)
        into = Rows(ext, edge)
        if j:
            state.halo()
            along_y(state, sides_ref, sums)
        series(slow, orders_ref[0, j], weights_ref, rates_ref, coefs_ref, j)

        def emit(r, b, re, im, j=j, into=into):
            for p, value in enumerate((re, im)):
                states_ref[j, p, r, :, b * LANES : (b + 1) * LANES] = value
                if j + 1 < steps:
                    into.put(p, r, b, value)
                else:
                    sent_ref[p, r, :, b * LANES : (b + 1) * LANES] = value

        depth_step(state, sums if j else sums_in, coefs_ref.at[j], 1, emit)


def first_image_kernel(
    sides_ref, ext_in, sums_in, coefs_ref, states_ref, image_ref, ext, sums
):
    steps = coefs_ref.shape[0]
    edge = sums.shape[0]
    into = Rows(ext, edge)
    for j in range(steps):
        state = into if j else Rows(ext_in, edge, 2, 2)
        if j:
            state.halo()
            along_y(state, sides_ref, sums)

        def emit(r, b, re, im, j=j):
            at = slice(b * LANES, (b + 1) * LANES)
            image_ref[j, r, :, at] = re * states_ref[j, 0, r, :, at] + im * states_ref[j, 1, r, :, at]
            if j + 1 < steps:
                into.put(0, r, b, re)
                into.put(1, r, b, im)

        depth_step(state, sums if j else sums_in, coefs_ref.at[j], -1, emit)


def take_rows(rows_ref, state):
    def body(r, _):
        for p in range(state.planes):
            for b in range(state.blocks):
                state.put(p, r, b, rows_ref[p, r, :, b * LANES : (b + 1) * LANES])
        return 0

    lax.fori_loop(0, state.R, body, 0, unroll=8)
    state.halo()


def receiver_kernel(
    axis, weights_ref, rates_ref, rows_any, rows_ref, t0, t1, t2, t3, sides_ref, coefs_ref,
    states_ref, words, words_sem, slow, coefs_up_ref, ext, sums
):
    copy = pltpu.make_async_copy(rows_any.at[0, rows_any.shape[1] - 1], words, words_sem)
    copy.start()
    steps = coefs_ref.shape[0]
    state = Rows(ext, sums.shape[0])
    take_rows(rows_ref, state)
    copy.wait()
    blocks = slow.shape[0]
    tiles = blocks * slow.shape[1] // t0.shape[2]
    for which, coefs in enumerate((coefs_up_ref, coefs_ref)):
        for j in range(steps):
            final = which == 1 and j == steps - 1
            if which == 0:
                first = j * (1 + tiles)

                def tile_of(a, b, first=first):
                    return words[0, first + 1 + a * blocks + b].astype(jnp.int32)

                place_tiles(axis, (t0, t1, t2, t3), tile_of, slow)
                order = words[0, first].astype(jnp.int32)
                series(slow, order, weights_ref, rates_ref, coefs, 0)

            def emit(r, b, re, im, j=j, which=which, final=final):
                for p, value in enumerate((re, im)):
                    if not final:
                        state.put(p, r, b, value)
                    if which == 1:
                        states_ref[j, p, r, :, b * LANES : (b + 1) * LANES] = value

            along_y(state, sides_ref, sums)
            depth_step(state, sums, coefs.at[j if which else 0], -1, emit)
            if not final:
                state.halo()


def source_kernel(
    rows_ref, coefs_ref, sides_ref, receivers_ref, image_ref, owners_ref, slots_ref,
    buffer_ref, state_ref, images, slot_rows, held, sem, slot_sem, ext, sums
):
    steps = coefs_ref.shape[0]
    state = Rows(ext, sums.shape[0])
    R = state.R
    take_rows(rows_ref, state)
    peers, _, size = buffer_ref.shape
    rows = (buffer_ref.shape[1] - slot_rows.shape[1]) // CAP
    tiles_x, tiles_y = images.shape[2] // rows, images.shape[1]
    copies = []

    def seat(p):
        j, a, b = p // (tiles_x * tiles_y), p // tiles_y % tiles_x, p % tiles_y
        owner = owners_ref[0, p]
        rank = jnp.int32(0)
        for before in range(p):
            rank = rank + (owners_ref[0, before] == owner).astype(jnp.int32)
        held[owner * CAP + rank] = slots_ref[0, p]
        copies.append(
            pltpu.make_async_copy(
                images.at[j, b, pl.ds(a * rows, rows)],
                buffer_ref.at[owner, pl.ds(pl.multiple_of(rank * rows, rows), rows)],
                sem.at[p],
            )
        )
        copies[-1].start()

    for o in range(peers * CAP):
        held[o] = -1
    for j in range(steps):
        final = j == steps - 1

        def emit(r, b, re, im, j=j, final=final):
            at = slice(b * LANES, (b + 1) * LANES)
            for p, value in enumerate((re, im)):
                if final:
                    state_ref[p, r, :, at] = value
                else:
                    state.put(p, r, b, value)
            images[j, b, pl.ds(r, SUBS, stride=R), :] = (
                image_ref[j, r, :, at]
                + re * receivers_ref[j, 0, r, :, at]
                + im * receivers_ref[j, 1, r, :, at]
            )

        along_y(state, sides_ref, sums)
        depth_step(state, sums, coefs_ref.at[j], 1, emit)
        for p in range(j * tiles_x * tiles_y, (j + 1) * tiles_x * tiles_y):
            seat(p)
        if not final:
            state.halo()
    lane = lax.broadcasted_iota(jnp.int32, slot_rows.shape[1:], 1)
    for o in range(peers):
        out = jnp.full(slot_rows.shape[1:], -1, jnp.int32)
        for i in range(CAP):
            out = jnp.where(lane == i, held[o * CAP + i], out)
        slot_rows[o] = out.astype(jnp.float32)
    last = pltpu.make_async_copy(
        slot_rows, buffer_ref.at[:, pl.ds(CAP * rows, slot_rows.shape[1])], slot_sem
    )
    last.start()
    for copy in copies:
        copy.wait()
    last.wait()


def output_kernel(source_ref, receivers_ref, out_ref, flat, sems):
    R = source_ref.shape[1]
    blocks = flat.shape[2]

    def body(r, _):
        for b in range(blocks):
            at = slice(b * LANES, (b + 1) * LANES)
            for p in (0, 1):
                flat[0, p, b, pl.ds(r, SUBS, stride=R), :] = source_ref[p, r, :, at]
                flat[1, p, b, pl.ds(r, SUBS, stride=R), :] = receivers_ref[receivers_ref.shape[0] - 1, p, r, :, at]
        return 0

    lax.fori_loop(0, R, body, 0, unroll=4)
    copies = [
        pltpu.make_async_copy(flat.at[:, :, b], out_ref.at[:, :, :, pl.ds(b * LANES, LANES)], sems.at[b])
        for b in range(blocks)
    ]
    for copy in copies:
        copy.start()
    for copy in copies:
        copy.wait()


def volume_kernel(received_ref, out_ref, slots, slot_sem, seats, sems):
    peers, rows, size = seats.shape
    first = pltpu.make_async_copy(received_ref.at[:, pl.ds(rows, 1)], slots, slot_sem)
    first.start()
    copies = []
    for s in range(peers):
        copies.append(
            pltpu.make_async_copy(received_ref.at[s, pl.ds(0, rows)], seats.at[s], sems.at[s])
        )
        copies[-1].start()
    out_ref[...] = jnp.zeros_like(out_ref)
    first.wait()
    for s in range(peers):
        copies[s].wait()
        for i in range(CAP):
            slot = slots[s, 0, i].astype(jnp.int32)

            @pl.when(slot >= 0)
            def _(s=s, i=i, slot=slot):
                out_ref[slot] += seats[s, i * size : (i + 1) * size, :]


def shifted(shard, axis, by):
    peers = lax.axis_size(axis)
    return lax.ppermute(shard, axis, [(i, i + by) for i in range(peers - by)])


def swapped(shard, axis, bits):
    return lax.ppermute(shard, axis, [(i, i ^ bits) for i in range(lax.axis_size(axis))])


def local(fields, vel_tiles, tile_ids, orders, term_weights, phase_rates, owners, image_slots):
    axis = "depth"
    peers = lax.axis_size(axis)
    cells_x, cells_y = fields.shape[3:]
    size = vel_tiles.shape[1]
    steps, tiles_x, tiles_y = tile_ids.shape[1:]
    terms = phase_rates.shape[0]
    R = cells_x // SUBS
    f32 = jnp.float32

    blocks = cells_y // LANES
    assert size == LANES and cells_x % SUBS == 0 and cells_y % LANES == 0

    edge = terms - 1
    sides = lane_sums(cells_y, terms)

    def flat(planes):
        return [pltpu.VMEM((planes, blocks, cells_x, LANES), f32), pltpu.SemaphoreType.DMA((blocks,))]

    def work(planes):
        return [
            pltpu.VMEM((planes, R + 2 * edge, SUBS, cells_y), f32),
            pltpu.VMEM((edge, 2, R + 2 * edge, SUBS, cells_y), f32),
        ]

    planes = (R, SUBS, cells_y)
    padded = (R + 2 * edge, SUBS, cells_y)
    call = partial(pl.pallas_call, compiler_params=PARAMS)
    ext, rows, source_sums, receiver_sums = call(
        rows_kernel,
        out_shape=(
            pltpu.VMEM((4,) + padded, f32),
            pltpu.VMEM((2, R + 1) + planes[1:], f32),
            pltpu.VMEM((edge, 2) + padded, f32),
            pltpu.VMEM((edge, 2) + padded, f32),
        ),
        in_specs=[SMEM] * 2 + [ANY, VMEM],
        out_specs=(VMEM,) * 4,
        scratch_shapes=flat(4) + [pltpu.SemaphoreType.DMA],
        name="rows",
    )(tile_ids, orders, in_hbm(fields.reshape(4, cells_x, cells_y)), sides)

    def stacked(parts):
        return call(
            stack_kernel,
            out_shape=pltpu.VMEM((len(parts),) + vel_tiles.shape, f32),
            in_specs=[ANY] * len(parts),
            out_specs=VMEM,
            scratch_shapes=[pltpu.SemaphoreType.DMA((len(parts),))],
            name="stack_tiles",
        )(*parts)

    line = [vel_tiles] + [swapped(vel_tiles, axis, 4 * i) for i in range(1, peers // 4)]
    across = [swapped(v, axis, 2) for v in line[:-1]]
    ext, rows, line[-1] = lax.optimization_barrier((ext, rows, line[-1]))
    across.append(swapped(line[-1], axis, 2))
    tiles = {0: stacked(line)}
    tiles[1] = swapped(tiles[0], axis, 1)
    tiles[2] = stacked(across)
    tiles[2], rows = lax.optimization_barrier((tiles[2], rows))
    tiles[3] = swapped(tiles[2], axis, 1)
    receiver_up = shifted(rows, axis, 1)
    ext, source_sums, receiver_sums = in_vmem(ext), in_vmem(source_sums), in_vmem(receiver_sums)
    tiles = [in_vmem(tiles[i]) for i in range(4)]
    slow = [pltpu.VMEM((blocks, cells_x, LANES), f32)]
    coefs, states, sent = call(
        partial(first_source_kernel, axis),
        out_shape=(
            pltpu.VMEM((steps, 2 * terms) + planes, f32),
            pltpu.VMEM((steps, 2) + planes, f32),
            pltpu.VMEM((2,) + planes, f32),
        ),
        in_specs=[SMEM] * 4 + [VMEM] * 7,
        out_specs=(VMEM, VMEM, VMEM),
        scratch_shapes=slow + work(2),
        name="first_sources",
    )(tile_ids, orders, term_weights, phase_rates, sides, ext, source_sums, *tiles)
    source_up = shifted(sent, axis, 1)
    coefs, states = in_vmem(coefs), in_vmem(states)
    image = call(
        first_image_kernel,
        out_shape=pltpu.VMEM((steps,) + planes, f32),
        in_specs=[VMEM] * 5,
        out_specs=VMEM,
        scratch_shapes=work(2),
        name="first_images",
    )(sides, ext, receiver_sums, coefs, states)
    image, receiver_up = lax.optimization_barrier((image, receiver_up))
    receivers = in_vmem(
        call(
            partial(receiver_kernel, axis),
            out_shape=pltpu.VMEM((steps, 2) + planes, f32),
            in_specs=[SMEM] * 2 + [ANY] + [VMEM] * 7,
            out_specs=VMEM,
            scratch_shapes=[pltpu.SMEM((SUBS, cells_y), f32), pltpu.SemaphoreType.DMA]
            + slow
            + [pltpu.VMEM((1, 2 * terms) + planes, f32)]
            + work(2),
            name="receiver_ticks",
        )(term_weights, phase_rates, receiver_up, in_vmem(receiver_up), *tiles, sides, coefs)
    )
    extra = SUBS
    buffer, source = call(
        source_kernel,
        out_shape=(
            pltpu.HBM((peers, CAP * size + extra, size), f32),
            pltpu.HBM((2,) + planes, f32),
        ),
        in_specs=[VMEM] * 5 + [SMEM] * 2,
        out_specs=(ANY, VMEM),
        scratch_shapes=[
            pltpu.VMEM((steps, blocks, cells_x, LANES), f32),
            pltpu.VMEM((peers, extra, size), f32),
            pltpu.SMEM((peers * CAP,), jnp.int32),
            pltpu.SemaphoreType.DMA((steps * tiles_x * tiles_y,)),
            pltpu.SemaphoreType.DMA,
        ]
        + work(2),
        name="source_tick_and_seats",
    )(in_vmem(source_up), coefs, sides, receivers, in_vmem(image), owners, image_slots)
    received = lax.all_to_all(buffer, axis, split_axis=0, concat_axis=0, tiled=True)
    wavefields = pl.pallas_call(
        output_kernel,
        out_shape=jax.ShapeDtypeStruct((2, 2, cells_x, cells_y), f32),
        in_specs=[VMEM, VMEM],
        out_specs=ANY,
        scratch_shapes=[
            pltpu.VMEM((2, 2, blocks, cells_x, LANES), f32),
            pltpu.SemaphoreType.DMA((blocks,)),
        ],
        compiler_params=PARAMS,
        name="wavefields",
    )(source, receivers)
    volume = call(
        volume_kernel,
        out_shape=jax.ShapeDtypeStruct((IMG_SLOTS, size, size), f32),
        in_specs=[ANY],
        out_specs=VMEM,
        scratch_shapes=[
            pltpu.SMEM((peers, 1, size), f32),
            pltpu.SemaphoreType.DMA,
            pltpu.VMEM((peers, CAP * size, size), f32),
            pltpu.SemaphoreType.DMA((peers,)),
        ],
        name="image_volume",
    )(received)
    return volume, wavefields[None]


def solution(mesh):
    placed = (
        P(("groups", "depth"), None, None, None, None),
        P(("groups", "depth"), None, None),
        P(("groups", "depth"), None, None, None),
        P(("groups", "depth"), None),
        P(),
        P(),
        P(("groups", "depth"), None),
        P(("groups", "depth"), None),
    )
    return jax.shard_map(
        local,
        mesh=mesh,
        in_specs=placed,
        out_specs=(
            P(("groups", "depth"), None, None),
            P(("groups", "depth"), None, None, None, None),
        ),
        check_vma=False,
    )
```

```python
from functools import partial

import jax
import jax.numpy as jnp
import numpy as np
from jax import lax
from jax.experimental import pallas as pl
from jax.experimental.pallas import tpu as pltpu
from jax.sharding import PartitionSpec as P

TICKS = 2
CAP = 2
IMG_SLOTS = 8
LANES = 128
SUBS = 8
VMEM = pl.BlockSpec(memory_space=pltpu.VMEM)
SMEM = pl.BlockSpec(memory_space=pltpu.SMEM)
ANY = pl.BlockSpec(memory_space=pl.ANY)
PARAMS = pltpu.CompilerParams(vmem_limit_bytes=14 * 2**20)


def in_vmem(x):
    return pltpu.with_memory_space_constraint(x, pltpu.VMEM)


def in_hbm(x):
    return pltpu.with_memory_space_constraint(x, pltpu.HBM)


def in_powers(terms):
    rows = np.zeros((terms, terms))
    polys = [np.array([1.0]), np.array([-1.0, 1.0])]
    while len(polys) < terms:
        grown = np.convolve(polys[-1], [-2.0, 2.0])
        grown[: len(polys[-2])] -= polys[-2]
        polys.append(grown)
    for k in range(terms):
        rows[k, : len(polys[k])] = polys[k] / 8.0 ** np.arange(len(polys[k]))
    lead = np.diag(rows).copy()
    return rows / lead, lead


def fitted():
    nodes = 0.25 * (1.0 - np.cos((np.arange(400) + 0.5) * np.pi / 400)) / 2.0
    r = np.sqrt(nodes)
    sine = np.polynomial.chebyshev.Chebyshev.fit(nodes, np.sqrt(2.0) * np.sin(np.pi * r) / r, 4)
    cosine = np.polynomial.chebyshev.Chebyshev.fit(nodes, np.sqrt(2.0) * np.cos(np.pi * r), 4)
    make = np.polynomial.polynomial.Polynomial
    return (
        [float(c) for c in sine.convert(kind=make).coef],
        [float(c) for c in cosine.convert(kind=make).coef],
    )


SINE, COSINE = fitted()
ROUNDER = 1.5 * 2.0**23


def horner(x, coefs):
    out = coefs[-1] * x + coefs[-2]
    for c in coefs[-3::-1]:
        out = out * x + c
    return out


def cos_sin(turns):
    r = turns - ((turns + ROUNDER) - ROUNDER)
    r2 = r * r
    s = r * horner(r2, SINE)
    c = horner(r2, COSINE)
    return 1.0 - s * s, s * c


def lane_sums(cells_y, terms):
    one = 2 * np.eye(cells_y) + np.eye(cells_y, k=1) + np.eye(cells_y, k=-1)
    _, lead = in_powers(terms)
    side = np.concatenate([lead[k] * np.linalg.matrix_power(one, k) for k in range(1, terms)], 1)
    return jnp.asarray(np.concatenate([side, side], 0), jnp.bfloat16)


class Rows:
    def __init__(self, ref, edge, first=0, planes=None):
        self.ref, self.edge, self.first = ref, edge, first
        self.planes = ref.shape[0] if planes is None else planes
        self.R = ref.shape[1] - 2 * edge
        self.blocks = ref.shape[3] // LANES

    def get(self, p, r, b):
        return self.ref[self.first + p, r + self.edge, :, b * LANES : (b + 1) * LANES]

    def put(self, p, r, b, value):
        self.ref[self.first + p, r + self.edge, :, b * LANES : (b + 1) * LANES] = value

    def halo(self):
        sub = lax.broadcasted_iota(jnp.int32, (SUBS, LANES), 0)
        R = self.R
        for p in range(self.planes):
            for b in range(self.blocks):
                for h in range(1, self.edge + 1):
                    low = 0.0 if h == 1 else -self.get(p, h - 2, b)
                    self.put(p, -h, b, jnp.where(sub == 0, low, pltpu.roll(self.get(p, R - h, b), 1, 0)))
                    high = 0.0 if h == 1 else -self.get(p, R + 1 - h, b)
                    turned = pltpu.roll(self.get(p, h - 1, b), SUBS - 1, 0)
                    self.put(p, R - 1 + h, b, jnp.where(sub == SUBS - 1, high, turned))


def along_y(state, sides_ref, sums):
    rows, cells_y = state.ref.shape[1], state.ref.shape[3]
    side = sides_ref[...]
    for p in range(state.planes):
        here = state.ref[state.first + p].reshape(rows * SUBS, cells_y)
        high = here.astype(jnp.bfloat16)
        low = (here - high.astype(jnp.float32)).astype(jnp.bfloat16)
        out = jnp.dot(jnp.concatenate([high, low], 1), side, preferred_element_type=jnp.float32)
        for k in range(sums.shape[0]):
            sums[k, p] = out[:, k * cells_y : (k + 1) * cells_y].reshape(rows, SUBS, cells_y)


def chained(carry, value, length):
    kept = []
    for c in carry:
        kept.append(value)
        value = value + c
    if len(carry) < length:
        kept.append(value)
    return kept, value


def warm(sums, p, k, edge, at):
    chain = []
    for r in range(-k, k):
        chain, _ = chained(chain, sums[k - 1, p, r + edge, :, at], 2 * k)
    return chain


def along_x(sums, edge):
    orders, planes, rows, _, cells_y = sums.shape
    pairs = [(k, p) for k in range(1, orders + 1) for p in range(planes)]
    for b in range(cells_y // LANES):
        at = slice(b * LANES, (b + 1) * LANES)

        def body(r, carry):
            kept = []
            for (k, p), chain in zip(pairs, carry):
                new, value = chained(chain, sums[k - 1, p, r + edge + k, :, at], 2 * k)
                sums[k - 1, p, r + edge, :, at] = value
                kept.append(new)
            return kept

        lax.fori_loop(
            0, rows - 2 * edge, body, [warm(sums, p, k, edge, at) for k, p in pairs], unroll=8
        )


def depth_step(state, sums, coefs, sign, emit, unroll=8, summed=False, done=None):
    terms, edge = sums.shape[0] + 1, state.edge
    for b in range(state.blocks):
        at = slice(b * LANES, (b + 1) * LANES)

        def body(r, carry):
            kept, total = [], [None, None]
            for k in range(terms):
                if k == 0:
                    re, im = state.get(0, r, b), state.get(1, r, b)
                else:
                    both = []
                    for p in (0, 1):
                        if summed:
                            both.append(sums[k - 1, p, r + edge, :, at])
                            continue
                        new, value = chained(
                            carry[2 * (k - 1) + p], sums[k - 1, p, r + edge + k, :, at], 2 * k
                        )
                        kept.append(new)
                        both.append(value)
                    re, im = both
                a, s = coefs[2 * k, r, :, at], coefs[2 * k + 1, r, :, at]
                x, y, u, v = a * re, a * im, s * im, s * re
                x, y = (x - u, y + v) if sign > 0 else (x + u, y - v)
                total = [x, y] if k == 0 else [total[0] + x, total[1] + y]
            emit(r, b, *total)
            return kept

        pairs = [] if summed else [(k, p) for k in range(1, terms) for p in (0, 1)]
        start = [warm(sums, p, k, edge, at) for k, p in pairs]
        lax.fori_loop(0, state.R, body, start, unroll=unroll)
        if done is not None:
            done(b)


def fetch(field_ref, flat, sem):
    copies = [
        pltpu.make_async_copy(field_ref.at[:, :, pl.ds(b * LANES, LANES)], flat.at[:, b], sem.at[b])
        for b in range(flat.shape[1])
    ]
    for copy in copies:
        copy.start()
    return copies


def load_rows(flat, state):
    def body(r, _):
        for p in range(state.planes):
            for b in range(state.blocks):
                state.put(p, r, b, flat[state.first + p, b, pl.ds(r, SUBS, stride=state.R), :])
        return 0

    lax.fori_loop(0, state.R, body, 0, unroll=4)
    state.halo()


def stack_kernel(*refs):
    parts, (out, sems) = refs[:-2], refs[-2:]
    copies = [pltpu.make_async_copy(part, out.at[i], sems.at[i]) for i, part in enumerate(parts)]
    for copy in copies:
        copy.start()
    for copy in copies:
        copy.wait()


def words_of(ids_ref, orders_ref):
    _, steps, tiles_x, tiles_y = ids_ref.shape
    for j in range(steps):
        yield orders_ref[0, j]
        for a in range(tiles_x):
            for b in range(tiles_y):
                yield ids_ref[0, j, a, b]


def place_tiles(axis, tiles, tile_of, slow):
    _, per, size, _ = tiles[0].shape
    me = lax.axis_index(axis)
    for a in range(slow.shape[1] // size):
        for b in range(slow.shape[0]):
            tile = tile_of(a, b)
            apart = tile // per ^ me
            for low, ref in enumerate(tiles):

                @pl.when((apart & 3) == low)
                def _(a=a, b=b, ref=ref, group=apart >> 2, tile=tile):
                    slow[b, a * size : (a + 1) * size, :] = ref[group, tile % per]


def rows_kernel(
    ids_ref, orders_ref, fields_ref, ext, rows, flat, flat_sem, sem
):
    arriving = fetch(fields_ref, flat, flat_sem)
    R = rows.shape[1] - 1
    edge = (ext.shape[1] - R) // 2
    lane = lax.broadcasted_iota(jnp.int32, rows.shape[2:], 1)
    words = jnp.zeros(rows.shape[2:], jnp.int32)
    for i, word in enumerate(words_of(ids_ref, orders_ref)):
        words = jnp.where(lane == i, word, words)
    for p in range(rows.shape[0]):
        rows[p, R] = words.astype(jnp.float32)
    for copy in arriving:
        copy.wait()
    load_rows(flat, Rows(ext, edge))
    copy = pltpu.make_async_copy(
        ext.at[pl.ds(2, 2), pl.ds(edge, R)], rows.at[:, pl.ds(0, R)], sem
    )
    copy.start()
    copy.wait()


def sums_kernel(ext, sides_ref, source_sums, receiver_sums):
    edge = source_sums.shape[0]
    for first, sums in ((0, source_sums), (2, receiver_sums)):
        along_y(Rows(ext, edge, first, 2), sides_ref, sums)
        along_x(sums, edge)


def series(slow, order, weights_ref, rates_ref, coefs_ref, j):
    terms = rates_ref.shape[0]
    powers, _ = in_powers(terms)
    R = coefs_ref.shape[2]
    total = weights_ref[0]
    for k in range(1, terms - 1):
        total = total + weights_ref[k]
    base = [1.0 - total] + [weights_ref[k] for k in range(terms - 1)]
    turn = [rates_ref[k] * (0.5 / np.pi) for k in range(terms)]
    scale = [jnp.where(k <= order, base[k], 0.0) for k in range(terms)]

    def row(r, _):
        for b in range(slow.shape[0]):
            at = slice(b * LANES, (b + 1) * LANES)
            here = slow[b, pl.ds(r, SUBS, stride=R), :]
            parts = []
            for k in range(terms):
                c, s = cos_sin(here * turn[k])
                parts.append((c * scale[k], s * scale[k]))
            for m in range(terms):
                for i in (0, 1):
                    out = None
                    for k in range(m, terms):
                        w = float(powers[k, m])
                        term = parts[k][i] if abs(w) == 1.0 else parts[k][i] * abs(w)
                        if out is None:
                            out = term if w > 0 else -term
                        else:
                            out = out + term if w > 0 else out - term
                    coefs_ref[j, 2 * m + i, r, :, at] = out
        return 0

    lax.fori_loop(0, R, row, 0, unroll=8)


def first_source_kernel(
    axis, ids_ref, orders_ref, weights_ref, rates_ref, sides_ref, ext_in, sums_in, t0, t1, t2, t3,
    coefs_ref, states_ref, sent_ref, slow, ext, sums
):
    steps = ids_ref.shape[1]
    for j in range(steps):
        place_tiles(axis, (t0, t1, t2, t3), lambda a, b, j=j: ids_ref[0, j, a, b], slow)
        edge = sums.shape[0]
        state = Rows(ext_in if j == 0 else ext, edge, 0, 2)
        into = Rows(ext, edge)
        if j:
            state.halo()
            along_y(state, sides_ref, sums)
        series(slow, orders_ref[0, j], weights_ref, rates_ref, coefs_ref, j)

        def emit(r, b, re, im, j=j, into=into):
            for p, value in enumerate((re, im)):
                states_ref[j, p, r, :, b * LANES : (b + 1) * LANES] = value
                if j + 1 < steps:
                    into.put(p, r, b, value)
                else:
                    sent_ref[p, r, :, b * LANES : (b + 1) * LANES] = value

        depth_step(state, sums if j else sums_in, coefs_ref.at[j], 1, emit, summed=j == 0)


def first_image_kernel(
    sides_ref, ext_in, sums_in, coefs_ref, states_ref, image_ref, ext, sums
):
    steps = coefs_ref.shape[0]
    edge = sums.shape[0]
    into = Rows(ext, edge)
    for j in range(steps):
        state = into if j else Rows(ext_in, edge, 2, 2)
        if j:
            state.halo()
            along_y(state, sides_ref, sums)

        def emit(r, b, re, im, j=j):
            at = slice(b * LANES, (b + 1) * LANES)
            image_ref[j, r, :, at] = re * states_ref[j, 0, r, :, at] + im * states_ref[j, 1, r, :, at]
            if j + 1 < steps:
                into.put(0, r, b, re)
                into.put(1, r, b, im)

        depth_step(state, sums if j else sums_in, coefs_ref.at[j], -1, emit, summed=j == 0)


def take_rows(rows_ref, state):
    def body(r, _):
        for p in range(state.planes):
            for b in range(state.blocks):
                state.put(p, r, b, rows_ref[p, r, :, b * LANES : (b + 1) * LANES])
        return 0

    lax.fori_loop(0, state.R, body, 0, unroll=8)
    state.halo()


def receiver_kernel(
    axis, weights_ref, rates_ref, rows_any, rows_ref, t0, t1, t2, t3, sides_ref, coefs_ref,
    states_ref, words, words_sem, slow, coefs_up_ref, ext, sums
):
    copy = pltpu.make_async_copy(rows_any.at[0, rows_any.shape[1] - 1], words, words_sem)
    copy.start()
    steps = coefs_ref.shape[0]
    state = Rows(ext, sums.shape[0])
    take_rows(rows_ref, state)
    copy.wait()
    blocks = slow.shape[0]
    tiles = blocks * slow.shape[1] // t0.shape[2]
    for which, coefs in enumerate((coefs_up_ref, coefs_ref)):
        for j in range(steps):
            final = which == 1 and j == steps - 1
            if which == 0:
                first = j * (1 + tiles)

                def tile_of(a, b, first=first):
                    return words[0, first + 1 + a * blocks + b].astype(jnp.int32)

                place_tiles(axis, (t0, t1, t2, t3), tile_of, slow)
                order = words[0, first].astype(jnp.int32)
                series(slow, order, weights_ref, rates_ref, coefs, 0)

            def emit(r, b, re, im, j=j, which=which, final=final):
                for p, value in enumerate((re, im)):
                    if not final:
                        state.put(p, r, b, value)
                    if which == 1:
                        states_ref[j, p, r, :, b * LANES : (b + 1) * LANES] = value

            along_y(state, sides_ref, sums)
            depth_step(state, sums, coefs.at[j if which else 0], -1, emit)
            if not final:
                state.halo()


def source_kernel(
    rows_ref, coefs_ref, sides_ref, receivers_ref, image_ref, owners_ref, slots_ref,
    buffer_ref, state_out, images, slot_rows, held, sem, slot_sem, state_sem, last_state, ext, sums
):
    steps = coefs_ref.shape[0]
    state = Rows(ext, sums.shape[0])
    R = state.R
    peers, _, size = buffer_ref.shape
    rows = (buffer_ref.shape[1] - slot_rows.shape[1]) // CAP
    tiles_x, tiles_y = images.shape[2] // rows, images.shape[1]
    take_rows(rows_ref, state)
    along_y(state, sides_ref, sums)
    for o in range(peers * CAP):
        held[o] = -1
    ranks = []
    for p in range(steps * tiles_x * tiles_y):
        rank = jnp.int32(0)
        for before in range(p):
            rank = rank + (owners_ref[0, before] == owners_ref[0, p]).astype(jnp.int32)
        held[owners_ref[0, p] * CAP + rank] = slots_ref[0, p]
        ranks.append(rank)
    lane = lax.broadcasted_iota(jnp.int32, slot_rows.shape[1:], 1)
    for o in range(peers):
        out = jnp.full(slot_rows.shape[1:], -1, jnp.int32)
        for i in range(CAP):
            out = jnp.where(lane == i, held[o * CAP + i], out)
        slot_rows[o] = out.astype(jnp.float32)
    copies = [
        pltpu.make_async_copy(
            slot_rows, buffer_ref.at[:, pl.ds(CAP * rows, slot_rows.shape[1])], slot_sem
        )
    ]
    copies[0].start()
    for j in range(steps):
        final = j == steps - 1

        def emit(r, b, re, im, j=j, final=final):
            at = slice(b * LANES, (b + 1) * LANES)
            for p, value in enumerate((re, im)):
                if final:
                    last_state[p, r, :, at] = value
                else:
                    state.put(p, r, b, value)
            images[j, b, pl.ds(r, SUBS, stride=R), :] = (
                image_ref[j, r, :, at]
                + re * receivers_ref[j, 0, r, :, at]
                + im * receivers_ref[j, 1, r, :, at]
            )

        def done(b, j=j, final=final):
            for a in range(tiles_x):
                p = (j * tiles_x + a) * tiles_y + b
                copies.append(
                    pltpu.make_async_copy(
                        images.at[j, b, pl.ds(a * rows, rows)],
                        buffer_ref.at[
                            owners_ref[0, p], pl.ds(pl.multiple_of(ranks[p] * rows, rows), rows)
                        ],
                        sem.at[p],
                    )
                )
                copies[-1].start()
            if final:
                at = pl.ds(b * LANES, LANES)
                copies.append(
                    pltpu.make_async_copy(
                        last_state.at[:, :, :, at], state_out.at[:, :, :, at], state_sem.at[b]
                    )
                )
                copies[-1].start()

        if j:
            state.halo()
            along_y(state, sides_ref, sums)
        depth_step(state, sums, coefs_ref.at[j], 1, emit, done=done)
    for copy in copies:
        copy.wait()


def output_kernel(source_ref, receivers_ref, out_ref, flat, sems):
    R = source_ref.shape[1]
    blocks = flat.shape[2]

    def body(r, _):
        for b in range(blocks):
            at = slice(b * LANES, (b + 1) * LANES)
            for p in (0, 1):
                flat[0, p, b, pl.ds(r, SUBS, stride=R), :] = source_ref[p, r, :, at]
                flat[1, p, b, pl.ds(r, SUBS, stride=R), :] = receivers_ref[receivers_ref.shape[0] - 1, p, r, :, at]
        return 0

    lax.fori_loop(0, R, body, 0, unroll=4)
    copies = [
        pltpu.make_async_copy(flat.at[:, :, b], out_ref.at[:, :, :, pl.ds(b * LANES, LANES)], sems.at[b])
        for b in range(blocks)
    ]
    for copy in copies:
        copy.start()
    for copy in copies:
        copy.wait()


def volume_kernel(received_ref, out_ref, slots, slot_sem, seats, sems):
    peers, rows, size = seats.shape
    first = pltpu.make_async_copy(received_ref.at[:, pl.ds(rows, 1)], slots, slot_sem)
    first.start()
    copies = []
    for s in range(peers):
        copies.append(
            pltpu.make_async_copy(received_ref.at[s, pl.ds(0, rows)], seats.at[s], sems.at[s])
        )
        copies[-1].start()
    out_ref[...] = jnp.zeros_like(out_ref)
    first.wait()
    for s in range(peers):
        copies[s].wait()
        for i in range(CAP):
            slot = slots[s, 0, i].astype(jnp.int32)

            @pl.when(slot >= 0)
            def _(s=s, i=i, slot=slot):
                out_ref[slot] += seats[s, i * size : (i + 1) * size, :]


def shifted(shard, axis, by):
    peers = lax.axis_size(axis)
    return lax.ppermute(shard, axis, [(i, i + by) for i in range(peers - by)])


def swapped(shard, axis, bits):
    return lax.ppermute(shard, axis, [(i, i ^ bits) for i in range(lax.axis_size(axis))])


def local(fields, vel_tiles, tile_ids, orders, term_weights, phase_rates, owners, image_slots):
    axis = "depth"
    peers = lax.axis_size(axis)
    cells_x, cells_y = fields.shape[3:]
    size = vel_tiles.shape[1]
    steps, tiles_x, tiles_y = tile_ids.shape[1:]
    terms = phase_rates.shape[0]
    R = cells_x // SUBS
    f32 = jnp.float32

    blocks = cells_y // LANES
    assert size == LANES and cells_x % SUBS == 0 and cells_y % LANES == 0

    edge = terms - 1
    sides = lane_sums(cells_y, terms)

    def flat(planes):
        return [pltpu.VMEM((planes, blocks, cells_x, LANES), f32), pltpu.SemaphoreType.DMA((blocks,))]

    def work(planes):
        return [
            pltpu.VMEM((planes, R + 2 * edge, SUBS, cells_y), f32),
            pltpu.VMEM((edge, 2, R + 2 * edge, SUBS, cells_y), f32),
        ]

    planes = (R, SUBS, cells_y)
    padded = (R + 2 * edge, SUBS, cells_y)
    call = partial(pl.pallas_call, compiler_params=PARAMS)
    ext, rows = call(
        rows_kernel,
        out_shape=(pltpu.VMEM((4,) + padded, f32), pltpu.VMEM((2, R + 1) + planes[1:], f32)),
        in_specs=[SMEM] * 2 + [ANY],
        out_specs=(VMEM, VMEM),
        scratch_shapes=flat(4) + [pltpu.SemaphoreType.DMA],
        name="rows",
    )(tile_ids, orders, in_hbm(fields.reshape(4, cells_x, cells_y)))

    def stacked(parts):
        return call(
            stack_kernel,
            out_shape=pltpu.VMEM((len(parts),) + vel_tiles.shape, f32),
            in_specs=[ANY] * len(parts),
            out_specs=VMEM,
            scratch_shapes=[pltpu.SemaphoreType.DMA((len(parts),))],
            name="stack_tiles",
        )(*parts)

    line = [vel_tiles] + [swapped(vel_tiles, axis, 4 * i) for i in range(1, peers // 4 - 1)]
    across = [swapped(vel_tiles, axis, 2)]
    ext, rows, across[0], *line[1:] = lax.optimization_barrier((ext, rows, across[0], *line[1:]))
    across += [swapped(v, axis, 2) for v in line[1:]]
    line.append(swapped(line[-1], axis, 4))
    ext = in_vmem(ext)
    source_sums, receiver_sums = call(
        sums_kernel,
        out_shape=(pltpu.VMEM((edge, 2) + padded, f32),) * 2,
        in_specs=[VMEM, VMEM],
        out_specs=(VMEM, VMEM),
        name="first_sums",
    )(ext, sides)
    line[-1], source_sums, receiver_sums = lax.optimization_barrier(
        (line[-1], source_sums, receiver_sums)
    )
    across.append(swapped(line[-1], axis, 2))
    tiles = {0: stacked(line)}
    tiles[1] = swapped(tiles[0], axis, 1)
    tiles[2] = stacked(across)
    tiles[2], rows = lax.optimization_barrier((tiles[2], rows))
    tiles[3] = swapped(tiles[2], axis, 1)
    receiver_up = shifted(rows, axis, 1)
    source_sums, receiver_sums = in_vmem(source_sums), in_vmem(receiver_sums)
    tiles = [in_vmem(tiles[i]) for i in range(4)]
    slow = [pltpu.VMEM((blocks, cells_x, LANES), f32)]
    coefs, states, sent = call(
        partial(first_source_kernel, axis),
        out_shape=(
            pltpu.VMEM((steps, 2 * terms) + planes, f32),
            pltpu.VMEM((steps, 2) + planes, f32),
            pltpu.VMEM((2,) + planes, f32),
        ),
        in_specs=[SMEM] * 4 + [VMEM] * 7,
        out_specs=(VMEM, VMEM, VMEM),
        scratch_shapes=slow + work(2),
        name="first_sources",
    )(tile_ids, orders, term_weights, phase_rates, sides, ext, source_sums, *tiles)
    source_up = shifted(sent, axis, 1)
    coefs, states = in_vmem(coefs), in_vmem(states)
    image = call(
        first_image_kernel,
        out_shape=pltpu.VMEM((steps,) + planes, f32),
        in_specs=[VMEM] * 5,
        out_specs=VMEM,
        scratch_shapes=work(2),
        name="first_images",
    )(sides, ext, receiver_sums, coefs, states)
    image, receiver_up = lax.optimization_barrier((image, receiver_up))
    receivers = in_vmem(
        call(
            partial(receiver_kernel, axis),
            out_shape=pltpu.VMEM((steps, 2) + planes, f32),
            in_specs=[SMEM] * 2 + [ANY] + [VMEM] * 7,
            out_specs=VMEM,
            scratch_shapes=[pltpu.SMEM((SUBS, cells_y), f32), pltpu.SemaphoreType.DMA]
            + slow
            + [pltpu.VMEM((1, 2 * terms) + planes, f32)]
            + work(2),
            name="receiver_ticks",
        )(term_weights, phase_rates, receiver_up, in_vmem(receiver_up), *tiles, sides, coefs)
    )
    extra = SUBS
    buffer, source = call(
        source_kernel,
        out_shape=(
            pltpu.HBM((peers, CAP * size + extra, size), f32),
            pltpu.HBM((2,) + planes, f32),
        ),
        in_specs=[VMEM] * 5 + [SMEM] * 2,
        out_specs=(ANY, ANY),
        scratch_shapes=[
            pltpu.VMEM((steps, blocks, cells_x, LANES), f32),
            pltpu.VMEM((peers, extra, size), f32),
            pltpu.SMEM((peers * CAP,), jnp.int32),
            pltpu.SemaphoreType.DMA((steps * tiles_x * tiles_y,)),
            pltpu.SemaphoreType.DMA,
            pltpu.SemaphoreType.DMA((blocks,)),
            pltpu.VMEM((2,) + planes, f32),
        ]
        + work(2),
        name="source_tick_and_seats",
    )(in_vmem(source_up), coefs, sides, receivers, in_vmem(image), owners, image_slots)
    received = lax.all_to_all(buffer, axis, split_axis=0, concat_axis=0, tiled=True)
    wavefields = pl.pallas_call(
        output_kernel,
        out_shape=jax.ShapeDtypeStruct((2, 2, cells_x, cells_y), f32),
        in_specs=[VMEM, VMEM],
        out_specs=ANY,
        scratch_shapes=[
            pltpu.VMEM((2, 2, blocks, cells_x, LANES), f32),
            pltpu.SemaphoreType.DMA((blocks,)),
        ],
        compiler_params=PARAMS,
        name="wavefields",
    )(source, receivers)
    volume = call(
        volume_kernel,
        out_shape=jax.ShapeDtypeStruct((IMG_SLOTS, size, size), f32),
        in_specs=[ANY],
        out_specs=VMEM,
        scratch_shapes=[
            pltpu.SMEM((peers, 1, size), f32),
            pltpu.SemaphoreType.DMA,
            pltpu.VMEM((peers, CAP * size, size), f32),
            pltpu.SemaphoreType.DMA((peers,)),
        ],
        name="image_volume",
    )(received)
    return volume, wavefields[None]


def solution(mesh):
    placed = (
        P(("groups", "depth"), None, None, None, None),
        P(("groups", "depth"), None, None),
        P(("groups", "depth"), None, None, None),
        P(("groups", "depth"), None),
        P(),
        P(),
        P(("groups", "depth"), None),
        P(("groups", "depth"), None),
    )
    return jax.shard_map(
        local,
        mesh=mesh,
        in_specs=placed,
        out_specs=(
            P(("groups", "depth"), None, None),
            P(("groups", "depth"), None, None, None, None),
        ),
        check_vma=False,
    )
```

```python
from functools import partial

import jax
import jax.numpy as jnp
import numpy as np
from jax import lax
from jax.experimental import pallas as pl
from jax.experimental.pallas import tpu as pltpu
from jax.sharding import PartitionSpec as P

TICKS = 2
CAP = 2
IMG_SLOTS = 8
LANES = 128
SUBS = 8
VMEM = pl.BlockSpec(memory_space=pltpu.VMEM)
SMEM = pl.BlockSpec(memory_space=pltpu.SMEM)
ANY = pl.BlockSpec(memory_space=pl.ANY)
PARAMS = pltpu.CompilerParams(vmem_limit_bytes=14 * 2**20)


def in_vmem(x):
    return pltpu.with_memory_space_constraint(x, pltpu.VMEM)


def in_hbm(x):
    return pltpu.with_memory_space_constraint(x, pltpu.HBM)


def in_powers(terms):
    rows = np.zeros((terms, terms))
    polys = [np.array([1.0]), np.array([-1.0, 1.0])]
    while len(polys) < terms:
        grown = np.convolve(polys[-1], [-2.0, 2.0])
        grown[: len(polys[-2])] -= polys[-2]
        polys.append(grown)
    for k in range(terms):
        rows[k, : len(polys[k])] = polys[k] / 8.0 ** np.arange(len(polys[k]))
    lead = np.diag(rows).copy()
    return rows / lead, lead


def fitted():
    nodes = 0.25 * (1.0 - np.cos((np.arange(400) + 0.5) * np.pi / 400)) / 2.0
    r = np.sqrt(nodes)
    sine = np.polynomial.chebyshev.Chebyshev.fit(nodes, np.sqrt(2.0) * np.sin(np.pi * r) / r, 4)
    cosine = np.polynomial.chebyshev.Chebyshev.fit(nodes, np.sqrt(2.0) * np.cos(np.pi * r), 4)
    make = np.polynomial.polynomial.Polynomial
    return (
        [float(c) for c in sine.convert(kind=make).coef],
        [float(c) for c in cosine.convert(kind=make).coef],
    )


SINE, COSINE = fitted()
ROUNDER = 1.5 * 2.0**23


def horner(x, coefs):
    out = coefs[-1] * x + coefs[-2]
    for c in coefs[-3::-1]:
        out = out * x + c
    return out


def cos_sin(turns):
    r = turns - ((turns + ROUNDER) - ROUNDER)
    r2 = r * r
    s = r * horner(r2, SINE)
    c = horner(r2, COSINE)
    return 1.0 - s * s, s * c


def lane_sums(cells_y, terms):
    one = 2 * np.eye(cells_y) + np.eye(cells_y, k=1) + np.eye(cells_y, k=-1)
    _, lead = in_powers(terms)
    side = np.concatenate([lead[k] * np.linalg.matrix_power(one, k) for k in range(1, terms)], 1)
    return jnp.asarray(np.concatenate([side, side], 0), jnp.bfloat16)


class Rows:
    def __init__(self, ref, edge, first=0, planes=None):
        self.ref, self.edge, self.first = ref, edge, first
        self.planes = ref.shape[0] if planes is None else planes
        self.R = ref.shape[1] - 2 * edge
        self.blocks = ref.shape[3] // LANES

    def get(self, p, r, b):
        return self.ref[self.first + p, r + self.edge, :, b * LANES : (b + 1) * LANES]

    def put(self, p, r, b, value):
        self.ref[self.first + p, r + self.edge, :, b * LANES : (b + 1) * LANES] = value

    def halo(self):
        sub = lax.broadcasted_iota(jnp.int32, (SUBS, LANES), 0)
        R = self.R
        for p in range(self.planes):
            for b in range(self.blocks):
                for h in range(1, self.edge + 1):
                    low = 0.0 if h == 1 else -self.get(p, h - 2, b)
                    self.put(p, -h, b, jnp.where(sub == 0, low, pltpu.roll(self.get(p, R - h, b), 1, 0)))
                    high = 0.0 if h == 1 else -self.get(p, R + 1 - h, b)
                    turned = pltpu.roll(self.get(p, h - 1, b), SUBS - 1, 0)
                    self.put(p, R - 1 + h, b, jnp.where(sub == SUBS - 1, high, turned))


def along_y(state, sides_ref, sums):
    rows, cells_y = state.ref.shape[1], state.ref.shape[3]
    side = sides_ref[...]
    for p in range(state.planes):
        here = state.ref[state.first + p].reshape(rows * SUBS, cells_y)
        high = here.astype(jnp.bfloat16)
        low = (here - high.astype(jnp.float32)).astype(jnp.bfloat16)
        out = jnp.dot(jnp.concatenate([high, low], 1), side, preferred_element_type=jnp.float32)
        for k in range(sums.shape[0]):
            sums[k, p] = out[:, k * cells_y : (k + 1) * cells_y].reshape(rows, SUBS, cells_y)


def chained(carry, value, length):
    kept = []
    for c in carry:
        kept.append(value)
        value = value + c
    if len(carry) < length:
        kept.append(value)
    return kept, value


def warm(sums, p, k, edge, at):
    chain = []
    for r in range(-k, k):
        chain, _ = chained(chain, sums[k - 1, p, r + edge, :, at], 2 * k)
    return chain


def along_x(sums, edge):
    orders, planes, rows, _, cells_y = sums.shape
    pairs = [(k, p) for k in range(1, orders + 1) for p in range(planes)]
    for b in range(cells_y // LANES):
        at = slice(b * LANES, (b + 1) * LANES)

        def body(r, carry):
            kept = []
            for (k, p), chain in zip(pairs, carry):
                new, value = chained(chain, sums[k - 1, p, r + edge + k, :, at], 2 * k)
                sums[k - 1, p, r + edge, :, at] = value
                kept.append(new)
            return kept

        lax.fori_loop(
            0, rows - 2 * edge, body, [warm(sums, p, k, edge, at) for k, p in pairs], unroll=8
        )


def depth_step(state, sums, coefs, sign, emit, unroll=16, summed=False, done=None):
    terms, edge = sums.shape[0] + 1, state.edge
    for b in range(state.blocks):
        at = slice(b * LANES, (b + 1) * LANES)

        def body(r, carry):
            kept, total = [], [None, None]
            for k in range(terms):
                if k == 0:
                    re, im = state.get(0, r, b), state.get(1, r, b)
                else:
                    both = []
                    for p in (0, 1):
                        if summed:
                            both.append(sums[k - 1, p, r + edge, :, at])
                            continue
                        new, value = chained(
                            carry[2 * (k - 1) + p], sums[k - 1, p, r + edge + k, :, at], 2 * k
                        )
                        kept.append(new)
                        both.append(value)
                    re, im = both
                a, s = coefs[2 * k, r, :, at], coefs[2 * k + 1, r, :, at]
                x, y, u, v = a * re, a * im, s * im, s * re
                x, y = (x - u, y + v) if sign > 0 else (x + u, y - v)
                total = [x, y] if k == 0 else [total[0] + x, total[1] + y]
            emit(r, b, *total)
            return kept

        pairs = [] if summed else [(k, p) for k in range(1, terms) for p in (0, 1)]
        start = [warm(sums, p, k, edge, at) for k, p in pairs]
        lax.fori_loop(0, state.R, body, start, unroll=unroll)
        if done is not None:
            done(b)


def fetch(field_ref, flat, sem):
    copies = [
        pltpu.make_async_copy(field_ref.at[:, :, pl.ds(b * LANES, LANES)], flat.at[:, b], sem.at[b])
        for b in range(flat.shape[1])
    ]
    for copy in copies:
        copy.start()
    return copies


def load_rows(flat, state):
    def body(r, _):
        for p in range(state.planes):
            for b in range(state.blocks):
                state.put(p, r, b, flat[state.first + p, b, pl.ds(r, SUBS, stride=state.R), :])
        return 0

    lax.fori_loop(0, state.R, body, 0, unroll=4)
    state.halo()


def stack_kernel(*refs):
    parts, (out, sems) = refs[:-2], refs[-2:]
    copies = [pltpu.make_async_copy(part, out.at[i], sems.at[i]) for i, part in enumerate(parts)]
    for copy in copies:
        copy.start()
    for copy in copies:
        copy.wait()


def words_of(ids_ref, orders_ref):
    _, steps, tiles_x, tiles_y = ids_ref.shape
    for j in range(steps):
        yield orders_ref[0, j]
        for a in range(tiles_x):
            for b in range(tiles_y):
                yield ids_ref[0, j, a, b]


def place_tiles(axis, tiles, tile_of, slow):
    _, per, size, _ = tiles[0].shape
    me = lax.axis_index(axis)
    for a in range(slow.shape[1] // size):
        for b in range(slow.shape[0]):
            tile = tile_of(a, b)
            apart = tile // per ^ me
            for low, ref in enumerate(tiles):

                @pl.when((apart & 3) == low)
                def _(a=a, b=b, ref=ref, group=apart >> 2, tile=tile):
                    slow[b, a * size : (a + 1) * size, :] = ref[group, tile % per]


def rows_kernel(
    ids_ref, orders_ref, fields_ref, ext, rows, flat, flat_sem, sem
):
    arriving = fetch(fields_ref, flat, flat_sem)
    R = rows.shape[1] - 1
    edge = (ext.shape[1] - R) // 2
    lane = lax.broadcasted_iota(jnp.int32, rows.shape[2:], 1)
    words = jnp.zeros(rows.shape[2:], jnp.int32)
    for i, word in enumerate(words_of(ids_ref, orders_ref)):
        words = jnp.where(lane == i, word, words)
    for p in range(rows.shape[0]):
        rows[p, R] = words.astype(jnp.float32)
    for copy in arriving:
        copy.wait()
    load_rows(flat, Rows(ext, edge))
    copy = pltpu.make_async_copy(
        ext.at[pl.ds(2, 2), pl.ds(edge, R)], rows.at[:, pl.ds(0, R)], sem
    )
    copy.start()
    copy.wait()


def sums_kernel(ext, sides_ref, source_sums, receiver_sums):
    edge = source_sums.shape[0]
    for first, sums in ((0, source_sums), (2, receiver_sums)):
        along_y(Rows(ext, edge, first, 2), sides_ref, sums)
        along_x(sums, edge)


def series(slow, order, weights_ref, rates_ref, coefs_ref, j):
    terms = rates_ref.shape[0]
    powers, _ = in_powers(terms)
    R = coefs_ref.shape[2]
    total = weights_ref[0]
    for k in range(1, terms - 1):
        total = total + weights_ref[k]
    base = [1.0 - total] + [weights_ref[k] for k in range(terms - 1)]
    turn = [rates_ref[k] * (0.5 / np.pi) for k in range(terms)]
    scale = [jnp.where(k <= order, base[k], 0.0) for k in range(terms)]

    def row(r, _):
        for b in range(slow.shape[0]):
            at = slice(b * LANES, (b + 1) * LANES)
            here = slow[b, pl.ds(r, SUBS, stride=R), :]
            parts = []
            for k in range(terms):
                c, s = cos_sin(here * turn[k])
                parts.append((c * scale[k], s * scale[k]))
            for m in range(terms):
                for i in (0, 1):
                    out = None
                    for k in range(m, terms):
                        w = float(powers[k, m])
                        term = parts[k][i] if abs(w) == 1.0 else parts[k][i] * abs(w)
                        if out is None:
                            out = term if w > 0 else -term
                        else:
                            out = out + term if w > 0 else out - term
                    coefs_ref[j, 2 * m + i, r, :, at] = out
        return 0

    lax.fori_loop(0, R, row, 0, unroll=8)


def first_source_kernel(
    axis, ids_ref, orders_ref, weights_ref, rates_ref, sides_ref, ext_in, sums_in, t0, t1, t2, t3,
    coefs_ref, states_ref, sent_ref, slow, ext, sums
):
    steps = ids_ref.shape[1]
    for j in range(steps):
        place_tiles(axis, (t0, t1, t2, t3), lambda a, b, j=j: ids_ref[0, j, a, b], slow)
        edge = sums.shape[0]
        state = Rows(ext_in if j == 0 else ext, edge, 0, 2)
        into = Rows(ext, edge)
        if j:
            state.halo()
            along_y(state, sides_ref, sums)
        series(slow, orders_ref[0, j], weights_ref, rates_ref, coefs_ref, j)

        def emit(r, b, re, im, j=j, into=into):
            for p, value in enumerate((re, im)):
                states_ref[j, p, r, :, b * LANES : (b + 1) * LANES] = value
                if j + 1 < steps:
                    into.put(p, r, b, value)
                else:
                    sent_ref[p, r, :, b * LANES : (b + 1) * LANES] = value

        depth_step(state, sums if j else sums_in, coefs_ref.at[j], 1, emit, summed=j == 0)


def first_image_kernel(
    sides_ref, ext_in, sums_in, coefs_ref, states_ref, image_ref, ext, sums
):
    steps = coefs_ref.shape[0]
    edge = sums.shape[0]
    into = Rows(ext, edge)
    for j in range(steps):
        state = into if j else Rows(ext_in, edge, 2, 2)
        if j:
            state.halo()
            along_y(state, sides_ref, sums)

        def emit(r, b, re, im, j=j):
            at = slice(b * LANES, (b + 1) * LANES)
            image_ref[j, r, :, at] = re * states_ref[j, 0, r, :, at] + im * states_ref[j, 1, r, :, at]
            if j + 1 < steps:
                into.put(0, r, b, re)
                into.put(1, r, b, im)

        depth_step(state, sums if j else sums_in, coefs_ref.at[j], -1, emit, summed=j == 0)


def take_rows(rows_ref, state):
    def body(r, _):
        for p in range(state.planes):
            for b in range(state.blocks):
                state.put(p, r, b, rows_ref[p, r, :, b * LANES : (b + 1) * LANES])
        return 0

    lax.fori_loop(0, state.R, body, 0, unroll=8)
    state.halo()


def receiver_kernel(
    axis, weights_ref, rates_ref, rows_any, rows_ref, t0, t1, t2, t3, sides_ref, coefs_ref,
    states_ref, words, words_sem, slow, coefs_up_ref, ext, sums
):
    copy = pltpu.make_async_copy(rows_any.at[0, rows_any.shape[1] - 1], words, words_sem)
    copy.start()
    steps = coefs_ref.shape[0]
    state = Rows(ext, sums.shape[0])
    take_rows(rows_ref, state)
    blocks = slow.shape[0]
    tiles = blocks * slow.shape[1] // t0.shape[2]
    for which, coefs in enumerate((coefs_up_ref, coefs_ref)):
        for j in range(steps):
            final = which == 1 and j == steps - 1
            along_y(state, sides_ref, sums)
            if which == 0 and j == 0:
                copy.wait()
            if which == 0:
                first = j * (1 + tiles)

                def tile_of(a, b, first=first):
                    return words[0, first + 1 + a * blocks + b].astype(jnp.int32)

                place_tiles(axis, (t0, t1, t2, t3), tile_of, slow)
                order = words[0, first].astype(jnp.int32)
                series(slow, order, weights_ref, rates_ref, coefs, 0)

            def emit(r, b, re, im, j=j, which=which, final=final):
                for p, value in enumerate((re, im)):
                    if not final:
                        state.put(p, r, b, value)
                    if which == 1:
                        states_ref[j, p, r, :, b * LANES : (b + 1) * LANES] = value

            depth_step(state, sums, coefs.at[j if which else 0], -1, emit)
            if not final:
                state.halo()


def source_kernel(
    rows_ref, coefs_ref, sides_ref, receivers_ref, image_ref, owners_ref, slots_ref,
    buffer_ref, state_out, images, slot_rows, held, sem, slot_sem, state_sem, last_state, ext, sums
):
    steps = coefs_ref.shape[0]
    state = Rows(ext, sums.shape[0])
    R = state.R
    peers, _, size = buffer_ref.shape
    rows = (buffer_ref.shape[1] - slot_rows.shape[1]) // CAP
    tiles_x, tiles_y = images.shape[2] // rows, images.shape[1]
    take_rows(rows_ref, state)
    along_y(state, sides_ref, sums)
    for o in range(peers * CAP):
        held[o] = -1
    ranks = []
    for p in range(steps * tiles_x * tiles_y):
        rank = jnp.int32(0)
        for before in range(p):
            rank = rank + (owners_ref[0, before] == owners_ref[0, p]).astype(jnp.int32)
        held[owners_ref[0, p] * CAP + rank] = slots_ref[0, p]
        ranks.append(rank)
    lane = lax.broadcasted_iota(jnp.int32, slot_rows.shape[1:], 1)
    for o in range(peers):
        out = jnp.full(slot_rows.shape[1:], -1, jnp.int32)
        for i in range(CAP):
            out = jnp.where(lane == i, held[o * CAP + i], out)
        slot_rows[o] = out.astype(jnp.float32)
    copies = [
        pltpu.make_async_copy(
            slot_rows, buffer_ref.at[:, pl.ds(CAP * rows, slot_rows.shape[1])], slot_sem
        )
    ]
    copies[0].start()
    for j in range(steps):
        final = j == steps - 1

        def emit(r, b, re, im, j=j, final=final):
            at = slice(b * LANES, (b + 1) * LANES)
            for p, value in enumerate((re, im)):
                if final:
                    last_state[p, r, :, at] = value
                else:
                    state.put(p, r, b, value)
            images[j, b, pl.ds(r, SUBS, stride=R), :] = (
                image_ref[j, r, :, at]
                + re * receivers_ref[j, 0, r, :, at]
                + im * receivers_ref[j, 1, r, :, at]
            )

        def done(b, j=j, final=final):
            for a in range(tiles_x):
                p = (j * tiles_x + a) * tiles_y + b
                copies.append(
                    pltpu.make_async_copy(
                        images.at[j, b, pl.ds(a * rows, rows)],
                        buffer_ref.at[
                            owners_ref[0, p], pl.ds(pl.multiple_of(ranks[p] * rows, rows), rows)
                        ],
                        sem.at[p],
                    )
                )
                copies[-1].start()
            if final:
                at = pl.ds(b * LANES, LANES)
                copies.append(
                    pltpu.make_async_copy(
                        last_state.at[:, :, :, at], state_out.at[:, :, :, at], state_sem.at[b]
                    )
                )
                copies[-1].start()

        if j:
            state.halo()
            along_y(state, sides_ref, sums)
        depth_step(state, sums, coefs_ref.at[j], 1, emit, done=done)
    for copy in copies:
        copy.wait()


def output_kernel(source_ref, receivers_ref, out_ref, flat, sems):
    R = source_ref.shape[1]
    blocks = flat.shape[2]

    def body(r, _):
        for b in range(blocks):
            at = slice(b * LANES, (b + 1) * LANES)
            for p in (0, 1):
                flat[0, p, b, pl.ds(r, SUBS, stride=R), :] = source_ref[p, r, :, at]
                flat[1, p, b, pl.ds(r, SUBS, stride=R), :] = receivers_ref[receivers_ref.shape[0] - 1, p, r, :, at]
        return 0

    lax.fori_loop(0, R, body, 0, unroll=4)
    copies = [
        pltpu.make_async_copy(flat.at[:, :, b], out_ref.at[:, :, :, pl.ds(b * LANES, LANES)], sems.at[b])
        for b in range(blocks)
    ]
    for copy in copies:
        copy.start()
    for copy in copies:
        copy.wait()


def volume_kernel(received_ref, out_ref, slots, slot_sem, seats, sems):
    peers, rows, size = seats.shape
    first = pltpu.make_async_copy(received_ref.at[:, pl.ds(rows, 1)], slots, slot_sem)
    first.start()
    copies = []
    for s in range(peers):
        copies.append(
            pltpu.make_async_copy(received_ref.at[s, pl.ds(0, rows)], seats.at[s], sems.at[s])
        )
        copies[-1].start()
    out_ref[...] = jnp.zeros_like(out_ref)
    first.wait()
    for s in range(peers):
        copies[s].wait()
        for i in range(CAP):
            slot = slots[s, 0, i].astype(jnp.int32)

            @pl.when(slot >= 0)
            def _(s=s, i=i, slot=slot):
                out_ref[slot] += seats[s, i * size : (i + 1) * size, :]


def shifted(shard, axis, by):
    peers = lax.axis_size(axis)
    return lax.ppermute(shard, axis, [(i, i + by) for i in range(peers - by)])


def swapped(shard, axis, bits):
    return lax.ppermute(shard, axis, [(i, i ^ bits) for i in range(lax.axis_size(axis))])


def local(fields, vel_tiles, tile_ids, orders, term_weights, phase_rates, owners, image_slots):
    axis = "depth"
    peers = lax.axis_size(axis)
    cells_x, cells_y = fields.shape[3:]
    size = vel_tiles.shape[1]
    steps, tiles_x, tiles_y = tile_ids.shape[1:]
    terms = phase_rates.shape[0]
    R = cells_x // SUBS
    f32 = jnp.float32

    blocks = cells_y // LANES
    assert size == LANES and cells_x % SUBS == 0 and cells_y % LANES == 0

    edge = terms - 1
    sides = lane_sums(cells_y, terms)

    def flat(planes):
        return [pltpu.VMEM((planes, blocks, cells_x, LANES), f32), pltpu.SemaphoreType.DMA((blocks,))]

    def work(planes):
        return [
            pltpu.VMEM((planes, R + 2 * edge, SUBS, cells_y), f32),
            pltpu.VMEM((edge, 2, R + 2 * edge, SUBS, cells_y), f32),
        ]

    planes = (R, SUBS, cells_y)
    padded = (R + 2 * edge, SUBS, cells_y)
    call = partial(pl.pallas_call, compiler_params=PARAMS)
    ext, rows = call(
        rows_kernel,
        out_shape=(pltpu.VMEM((4,) + padded, f32), pltpu.VMEM((2, R + 1) + planes[1:], f32)),
        in_specs=[SMEM] * 2 + [ANY],
        out_specs=(VMEM, VMEM),
        scratch_shapes=flat(4) + [pltpu.SemaphoreType.DMA],
        name="rows",
    )(tile_ids, orders, in_hbm(fields.reshape(4, cells_x, cells_y)))

    def stacked(parts):
        return call(
            stack_kernel,
            out_shape=pltpu.VMEM((len(parts),) + vel_tiles.shape, f32),
            in_specs=[ANY] * len(parts),
            out_specs=VMEM,
            scratch_shapes=[pltpu.SemaphoreType.DMA((len(parts),))],
            name="stack_tiles",
        )(*parts)

    line = [vel_tiles] + [swapped(vel_tiles, axis, 4 * i) for i in range(1, peers // 4 - 1)]
    across = [swapped(vel_tiles, axis, 2)]
    ext, rows, across[0], *line[1:] = lax.optimization_barrier((ext, rows, across[0], *line[1:]))
    across += [swapped(v, axis, 2) for v in line[1:]]
    line.append(swapped(line[-1], axis, 4))
    ext = in_vmem(ext)
    source_sums, receiver_sums = call(
        sums_kernel,
        out_shape=(pltpu.VMEM((edge, 2) + padded, f32),) * 2,
        in_specs=[VMEM, VMEM],
        out_specs=(VMEM, VMEM),
        name="first_sums",
    )(ext, sides)
    line[-1], source_sums, receiver_sums = lax.optimization_barrier(
        (line[-1], source_sums, receiver_sums)
    )
    across.append(swapped(line[-1], axis, 2))
    tiles = {0: stacked(line)}
    tiles[1] = swapped(tiles[0], axis, 1)
    tiles[2] = stacked(across)
    tiles[2], rows = lax.optimization_barrier((tiles[2], rows))
    tiles[3] = swapped(tiles[2], axis, 1)
    receiver_up = shifted(rows, axis, 1)
    source_sums, receiver_sums = in_vmem(source_sums), in_vmem(receiver_sums)
    tiles = [in_vmem(tiles[i]) for i in range(4)]
    slow = [pltpu.VMEM((blocks, cells_x, LANES), f32)]
    coefs, states, sent = call(
        partial(first_source_kernel, axis),
        out_shape=(
            pltpu.VMEM((steps, 2 * terms) + planes, f32),
            pltpu.VMEM((steps, 2) + planes, f32),
            pltpu.VMEM((2,) + planes, f32),
        ),
        in_specs=[SMEM] * 4 + [VMEM] * 7,
        out_specs=(VMEM, VMEM, VMEM),
        scratch_shapes=slow + work(2),
        name="first_sources",
    )(tile_ids, orders, term_weights, phase_rates, sides, ext, source_sums, *tiles)
    source_up = shifted(sent, axis, 1)
    coefs, states = in_vmem(coefs), in_vmem(states)
    image = call(
        first_image_kernel,
        out_shape=pltpu.VMEM((steps,) + planes, f32),
        in_specs=[VMEM] * 5,
        out_specs=VMEM,
        scratch_shapes=work(2),
        name="first_images",
    )(sides, ext, receiver_sums, coefs, states)
    image, receiver_up = lax.optimization_barrier((image, receiver_up))
    receivers = in_vmem(
        call(
            partial(receiver_kernel, axis),
            out_shape=pltpu.VMEM((steps, 2) + planes, f32),
            in_specs=[SMEM] * 2 + [ANY] + [VMEM] * 7,
            out_specs=VMEM,
            scratch_shapes=[pltpu.SMEM((SUBS, cells_y), f32), pltpu.SemaphoreType.DMA]
            + slow
            + [pltpu.VMEM((1, 2 * terms) + planes, f32)]
            + work(2),
            name="receiver_ticks",
        )(term_weights, phase_rates, receiver_up, in_vmem(receiver_up), *tiles, sides, coefs)
    )
    extra = SUBS
    buffer, source = call(
        source_kernel,
        out_shape=(
            pltpu.HBM((peers, CAP * size + extra, size), f32),
            pltpu.HBM((2,) + planes, f32),
        ),
        in_specs=[VMEM] * 5 + [SMEM] * 2,
        out_specs=(ANY, ANY),
        scratch_shapes=[
            pltpu.VMEM((steps, blocks, cells_x, LANES), f32),
            pltpu.VMEM((peers, extra, size), f32),
            pltpu.SMEM((peers * CAP,), jnp.int32),
            pltpu.SemaphoreType.DMA((steps * tiles_x * tiles_y,)),
            pltpu.SemaphoreType.DMA,
            pltpu.SemaphoreType.DMA((blocks,)),
            pltpu.VMEM((2,) + planes, f32),
        ]
        + work(2),
        name="source_tick_and_seats",
    )(in_vmem(source_up), coefs, sides, receivers, in_vmem(image), owners, image_slots)
    received = lax.all_to_all(buffer, axis, split_axis=0, concat_axis=0, tiled=True)
    wavefields = pl.pallas_call(
        output_kernel,
        out_shape=jax.ShapeDtypeStruct((2, 2, cells_x, cells_y), f32),
        in_specs=[VMEM, VMEM],
        out_specs=ANY,
        scratch_shapes=[
            pltpu.VMEM((2, 2, blocks, cells_x, LANES), f32),
            pltpu.SemaphoreType.DMA((blocks,)),
        ],
        compiler_params=PARAMS,
        name="wavefields",
    )(source, receivers)
    volume = call(
        volume_kernel,
        out_shape=jax.ShapeDtypeStruct((IMG_SLOTS, size, size), f32),
        in_specs=[ANY],
        out_specs=VMEM,
        scratch_shapes=[
            pltpu.SMEM((peers, 1, size), f32),
            pltpu.SemaphoreType.DMA,
            pltpu.VMEM((peers, CAP * size, size), f32),
            pltpu.SemaphoreType.DMA((peers,)),
        ],
        name="image_volume",
    )(received)
    return volume, wavefields[None]


def solution(mesh):
    placed = (
        P(("groups", "depth"), None, None, None, None),
        P(("groups", "depth"), None, None),
        P(("groups", "depth"), None, None, None),
        P(("groups", "depth"), None),
        P(),
        P(),
        P(("groups", "depth"), None),
        P(("groups", "depth"), None),
    )
    return jax.shard_map(
        local,
        mesh=mesh,
        in_specs=placed,
        out_specs=(
            P(("groups", "depth"), None, None),
            P(("groups", "depth"), None, None, None, None),
        ),
        check_vma=False,
    )
```

```python
from functools import partial

import jax
import jax.numpy as jnp
import numpy as np
from jax import lax
from jax.experimental import pallas as pl
from jax.experimental.pallas import tpu as pltpu
from jax.sharding import PartitionSpec as P

TICKS = 2
CAP = 2
IMG_SLOTS = 8
LANES = 128
SUBS = 8
VMEM = pl.BlockSpec(memory_space=pltpu.VMEM)
SMEM = pl.BlockSpec(memory_space=pltpu.SMEM)
ANY = pl.BlockSpec(memory_space=pl.ANY)
PARAMS = pltpu.CompilerParams(vmem_limit_bytes=14 * 2**20)


def in_vmem(x):
    return pltpu.with_memory_space_constraint(x, pltpu.VMEM)


def in_hbm(x):
    return pltpu.with_memory_space_constraint(x, pltpu.HBM)


def in_powers(terms):
    rows = np.zeros((terms, terms))
    polys = [np.array([1.0]), np.array([-1.0, 1.0])]
    while len(polys) < terms:
        grown = np.convolve(polys[-1], [-2.0, 2.0])
        grown[: len(polys[-2])] -= polys[-2]
        polys.append(grown)
    for k in range(terms):
        rows[k, : len(polys[k])] = polys[k] / 8.0 ** np.arange(len(polys[k]))
    lead = np.diag(rows).copy()
    return rows / lead, lead


def fitted():
    nodes = 0.25 * (1.0 - np.cos((np.arange(400) + 0.5) * np.pi / 400)) / 2.0
    r = np.sqrt(nodes)
    sine = np.polynomial.chebyshev.Chebyshev.fit(nodes, np.sqrt(2.0) * np.sin(np.pi * r) / r, 4)
    cosine = np.polynomial.chebyshev.Chebyshev.fit(nodes, np.sqrt(2.0) * np.cos(np.pi * r), 4)
    make = np.polynomial.polynomial.Polynomial
    return (
        [float(c) for c in sine.convert(kind=make).coef],
        [float(c) for c in cosine.convert(kind=make).coef],
    )


SINE, COSINE = fitted()
ROUNDER = 1.5 * 2.0**23


def horner(x, coefs):
    out = coefs[-1] * x + coefs[-2]
    for c in coefs[-3::-1]:
        out = out * x + c
    return out


def cos_sin(turns):
    r = turns - ((turns + ROUNDER) - ROUNDER)
    r2 = r * r
    s = r * horner(r2, SINE)
    c = horner(r2, COSINE)
    return 1.0 - s * s, s * c


def lane_sums(cells_y, terms):
    one = 2 * np.eye(cells_y) + np.eye(cells_y, k=1) + np.eye(cells_y, k=-1)
    _, lead = in_powers(terms)
    side = np.concatenate([lead[k] * np.linalg.matrix_power(one, k) for k in range(1, terms)], 1)
    return jnp.asarray(np.concatenate([side, side], 0), jnp.bfloat16)


class Rows:
    def __init__(self, ref, edge, first=0, planes=None):
        self.ref, self.edge, self.first = ref, edge, first
        self.planes = ref.shape[0] if planes is None else planes
        self.R = ref.shape[1] - 2 * edge
        self.blocks = ref.shape[3] // LANES

    def get(self, p, r, b):
        return self.ref[self.first + p, r + self.edge, :, b * LANES : (b + 1) * LANES]

    def put(self, p, r, b, value):
        self.ref[self.first + p, r + self.edge, :, b * LANES : (b + 1) * LANES] = value

    def halo(self):
        sub = lax.broadcasted_iota(jnp.int32, (SUBS, LANES), 0)
        R = self.R
        for p in range(self.planes):
            for b in range(self.blocks):
                for h in range(1, self.edge + 1):
                    low = 0.0 if h == 1 else -self.get(p, h - 2, b)
                    self.put(p, -h, b, jnp.where(sub == 0, low, pltpu.roll(self.get(p, R - h, b), 1, 0)))
                    high = 0.0 if h == 1 else -self.get(p, R + 1 - h, b)
                    turned = pltpu.roll(self.get(p, h - 1, b), SUBS - 1, 0)
                    self.put(p, R - 1 + h, b, jnp.where(sub == SUBS - 1, high, turned))


def along_y(state, sides_ref, sums):
    rows, cells_y = state.ref.shape[1], state.ref.shape[3]
    side = sides_ref[...]
    for p in range(state.planes):
        here = state.ref[state.first + p].reshape(rows * SUBS, cells_y)
        high = here.astype(jnp.bfloat16)
        low = (here - high.astype(jnp.float32)).astype(jnp.bfloat16)
        out = jnp.dot(jnp.concatenate([high, low], 1), side, preferred_element_type=jnp.float32)
        for k in range(sums.shape[0]):
            sums[k, p] = out[:, k * cells_y : (k + 1) * cells_y].reshape(rows, SUBS, cells_y)


def chained(carry, value, length):
    kept = []
    for c in carry:
        kept.append(value)
        value = value + c
    if len(carry) < length:
        kept.append(value)
    return kept, value


def warm(sums, p, k, edge, at):
    chain = []
    for r in range(-k, k):
        chain, _ = chained(chain, sums[k - 1, p, r + edge, :, at], 2 * k)
    return chain


def along_x(sums, edge):
    orders, planes, rows, _, cells_y = sums.shape
    pairs = [(k, p) for k in range(1, orders + 1) for p in range(planes)]
    for b in range(cells_y // LANES):
        at = slice(b * LANES, (b + 1) * LANES)

        def body(r, carry):
            kept = []
            for (k, p), chain in zip(pairs, carry):
                new, value = chained(chain, sums[k - 1, p, r + edge + k, :, at], 2 * k)
                sums[k - 1, p, r + edge, :, at] = value
                kept.append(new)
            return kept

        lax.fori_loop(
            0, rows - 2 * edge, body, [warm(sums, p, k, edge, at) for k, p in pairs], unroll=8
        )


def depth_step(state, sums, coefs, sign, emit, unroll=16, summed=False, done=None):
    terms, edge = sums.shape[0] + 1, state.edge
    for b in range(state.blocks):
        at = slice(b * LANES, (b + 1) * LANES)

        def body(r, carry):
            kept, total = [], [None, None]
            for k in range(terms):
                if k == 0:
                    re, im = state.get(0, r, b), state.get(1, r, b)
                else:
                    both = []
                    for p in (0, 1):
                        if summed:
                            both.append(sums[k - 1, p, r + edge, :, at])
                            continue
                        new, value = chained(
                            carry[2 * (k - 1) + p], sums[k - 1, p, r + edge + k, :, at], 2 * k
                        )
                        kept.append(new)
                        both.append(value)
                    re, im = both
                a, s = coefs[2 * k, r, :, at], coefs[2 * k + 1, r, :, at]
                x, y, u, v = a * re, a * im, s * im, s * re
                x, y = (x - u, y + v) if sign > 0 else (x + u, y - v)
                total = [x, y] if k == 0 else [total[0] + x, total[1] + y]
            emit(r, b, *total)
            return kept

        pairs = [] if summed else [(k, p) for k in range(1, terms) for p in (0, 1)]
        start = [warm(sums, p, k, edge, at) for k, p in pairs]
        lax.fori_loop(0, state.R, body, start, unroll=unroll)
        if done is not None:
            done(b)


def fetch(field_ref, flat, sem):
    copies = [
        pltpu.make_async_copy(field_ref.at[:, :, pl.ds(b * LANES, LANES)], flat.at[:, b], sem.at[b])
        for b in range(flat.shape[1])
    ]
    for copy in copies:
        copy.start()
    return copies


def load_rows(flat, state):
    def body(r, _):
        for p in range(state.planes):
            for b in range(state.blocks):
                state.put(p, r, b, flat[state.first + p, b, pl.ds(r, SUBS, stride=state.R), :])
        return 0

    lax.fori_loop(0, state.R, body, 0, unroll=4)
    state.halo()


def stack_kernel(*refs):
    parts, (out, sems) = refs[:-2], refs[-2:]
    copies = [pltpu.make_async_copy(part, out.at[i], sems.at[i]) for i, part in enumerate(parts)]
    for copy in copies:
        copy.start()
    for copy in copies:
        copy.wait()


def words_of(ids_ref, orders_ref):
    _, steps, tiles_x, tiles_y = ids_ref.shape
    for j in range(steps):
        yield orders_ref[0, j]
        for a in range(tiles_x):
            for b in range(tiles_y):
                yield ids_ref[0, j, a, b]


def place_tiles(axis, tiles, tile_of, slow):
    _, per, size, _ = tiles[0].shape
    me = lax.axis_index(axis)
    for a in range(slow.shape[1] // size):
        for b in range(slow.shape[0]):
            tile = tile_of(a, b)
            apart = tile // per ^ me
            for low, ref in enumerate(tiles):

                @pl.when((apart & 3) == low)
                def _(a=a, b=b, ref=ref, group=apart >> 2, tile=tile):
                    slow[b, a * size : (a + 1) * size, :] = ref[group, tile % per]


def rows_kernel(
    ids_ref, orders_ref, fields_ref, ext, rows, flat, flat_sem, sem
):
    arriving = fetch(fields_ref, flat, flat_sem)
    R = rows.shape[1] - 1
    edge = (ext.shape[1] - R) // 2
    lane = lax.broadcasted_iota(jnp.int32, rows.shape[2:], 1)
    words = jnp.zeros(rows.shape[2:], jnp.int32)
    for i, word in enumerate(words_of(ids_ref, orders_ref)):
        words = jnp.where(lane == i, word, words)
    for p in range(rows.shape[0]):
        rows[p, R] = words.astype(jnp.float32)
    for copy in arriving:
        copy.wait()
    load_rows(flat, Rows(ext, edge))
    copy = pltpu.make_async_copy(
        ext.at[pl.ds(2, 2), pl.ds(edge, R)], rows.at[:, pl.ds(0, R)], sem
    )
    copy.start()
    copy.wait()


def sums_kernel(first, ext, sides_ref, sums):
    edge = sums.shape[0]
    along_y(Rows(ext, edge, first, 2), sides_ref, sums)
    along_x(sums, edge)


def series(slow, order, weights_ref, rates_ref, coefs_ref, j):
    terms = rates_ref.shape[0]
    powers, _ = in_powers(terms)
    R = coefs_ref.shape[2]
    total = weights_ref[0]
    for k in range(1, terms - 1):
        total = total + weights_ref[k]
    base = [1.0 - total] + [weights_ref[k] for k in range(terms - 1)]
    turn = [rates_ref[k] * (0.5 / np.pi) for k in range(terms)]
    scale = [jnp.where(k <= order, base[k], 0.0) for k in range(terms)]

    def row(r, _):
        for b in range(slow.shape[0]):
            at = slice(b * LANES, (b + 1) * LANES)
            here = slow[b, pl.ds(r, SUBS, stride=R), :]
            parts = []
            for k in range(terms):
                c, s = cos_sin(here * turn[k])
                parts.append((c * scale[k], s * scale[k]))
            for m in range(terms):
                for i in (0, 1):
                    out = None
                    for k in range(m, terms):
                        w = float(powers[k, m])
                        term = parts[k][i] if abs(w) == 1.0 else parts[k][i] * abs(w)
                        if out is None:
                            out = term if w > 0 else -term
                        else:
                            out = out + term if w > 0 else out - term
                    coefs_ref[j, 2 * m + i, r, :, at] = out
        return 0

    lax.fori_loop(0, R, row, 0, unroll=8)


def first_source_kernel(
    axis, ids_ref, orders_ref, weights_ref, rates_ref, sides_ref, ext_in, sums_in, t0, t1, t2, t3,
    coefs_ref, states_ref, sent_ref, slow, ext, sums
):
    steps = ids_ref.shape[1]
    for j in range(steps):
        place_tiles(axis, (t0, t1, t2, t3), lambda a, b, j=j: ids_ref[0, j, a, b], slow)
        edge = sums.shape[0]
        state = Rows(ext_in if j == 0 else ext, edge, 0, 2)
        into = Rows(ext, edge)
        if j:
            state.halo()
            along_y(state, sides_ref, sums)
        series(slow, orders_ref[0, j], weights_ref, rates_ref, coefs_ref, j)

        def emit(r, b, re, im, j=j, into=into):
            for p, value in enumerate((re, im)):
                states_ref[j, p, r, :, b * LANES : (b + 1) * LANES] = value
                if j + 1 < steps:
                    into.put(p, r, b, value)
                else:
                    sent_ref[p, r, :, b * LANES : (b + 1) * LANES] = value

        depth_step(state, sums if j else sums_in, coefs_ref.at[j], 1, emit, summed=j == 0)


def first_image_kernel(
    sides_ref, ext_in, sums_in, coefs_ref, states_ref, image_ref, ext, sums
):
    steps = coefs_ref.shape[0]
    edge = sums.shape[0]
    into = Rows(ext, edge)
    for j in range(steps):
        state = into if j else Rows(ext_in, edge, 2, 2)
        if j:
            state.halo()
            along_y(state, sides_ref, sums)

        def emit(r, b, re, im, j=j):
            at = slice(b * LANES, (b + 1) * LANES)
            image_ref[j, r, :, at] = re * states_ref[j, 0, r, :, at] + im * states_ref[j, 1, r, :, at]
            if j + 1 < steps:
                into.put(0, r, b, re)
                into.put(1, r, b, im)

        depth_step(state, sums if j else sums_in, coefs_ref.at[j], -1, emit, summed=j == 0)


def take_rows(rows_ref, state):
    def body(r, _):
        for p in range(state.planes):
            for b in range(state.blocks):
                state.put(p, r, b, rows_ref[p, r, :, b * LANES : (b + 1) * LANES])
        return 0

    lax.fori_loop(0, state.R, body, 0, unroll=8)
    state.halo()


def receiver_kernel(
    axis, weights_ref, rates_ref, rows_any, rows_ref, t0, t1, t2, t3, sides_ref, coefs_ref,
    states_ref, words, words_sem, slow, coefs_up_ref, ext, sums
):
    copy = pltpu.make_async_copy(rows_any.at[0, rows_any.shape[1] - 1], words, words_sem)
    copy.start()
    steps = coefs_ref.shape[0]
    state = Rows(ext, sums.shape[0])
    take_rows(rows_ref, state)
    blocks = slow.shape[0]
    tiles = blocks * slow.shape[1] // t0.shape[2]
    for which, coefs in enumerate((coefs_up_ref, coefs_ref)):
        for j in range(steps):
            final = which == 1 and j == steps - 1
            along_y(state, sides_ref, sums)
            if which == 0 and j == 0:
                copy.wait()
            if which == 0:
                first = j * (1 + tiles)

                def tile_of(a, b, first=first):
                    return words[0, first + 1 + a * blocks + b].astype(jnp.int32)

                place_tiles(axis, (t0, t1, t2, t3), tile_of, slow)
                order = words[0, first].astype(jnp.int32)
                series(slow, order, weights_ref, rates_ref, coefs, 0)

            def emit(r, b, re, im, j=j, which=which, final=final):
                for p, value in enumerate((re, im)):
                    if not final:
                        state.put(p, r, b, value)
                    if which == 1:
                        states_ref[j, p, r, :, b * LANES : (b + 1) * LANES] = value

            depth_step(state, sums, coefs.at[j if which else 0], -1, emit)
            if not final:
                state.halo()


def source_kernel(
    rows_ref, coefs_ref, sides_ref, receivers_ref, image_ref, owners_ref, slots_ref,
    buffer_ref, state_out, images, slot_rows, held, sem, slot_sem, state_sem, last_state, ext, sums
):
    steps = coefs_ref.shape[0]
    state = Rows(ext, sums.shape[0])
    R = state.R
    peers, _, size = buffer_ref.shape
    rows = (buffer_ref.shape[1] - slot_rows.shape[1]) // CAP
    tiles_x, tiles_y = images.shape[2] // rows, images.shape[1]
    take_rows(rows_ref, state)
    along_y(state, sides_ref, sums)
    for o in range(peers * CAP):
        held[o] = -1
    ranks = []
    for p in range(steps * tiles_x * tiles_y):
        rank = jnp.int32(0)
        for before in range(p):
            rank = rank + (owners_ref[0, before] == owners_ref[0, p]).astype(jnp.int32)
        held[owners_ref[0, p] * CAP + rank] = slots_ref[0, p]
        ranks.append(rank)
    lane = lax.broadcasted_iota(jnp.int32, slot_rows.shape[1:], 1)
    for o in range(peers):
        out = jnp.full(slot_rows.shape[1:], -1, jnp.int32)
        for i in range(CAP):
            out = jnp.where(lane == i, held[o * CAP + i], out)
        slot_rows[o] = out.astype(jnp.float32)
    copies = [
        pltpu.make_async_copy(
            slot_rows, buffer_ref.at[:, pl.ds(CAP * rows, slot_rows.shape[1])], slot_sem
        )
    ]
    copies[0].start()
    for j in range(steps):
        final = j == steps - 1

        def emit(r, b, re, im, j=j, final=final):
            at = slice(b * LANES, (b + 1) * LANES)
            for p, value in enumerate((re, im)):
                if final:
                    last_state[p, r, :, at] = value
                else:
                    state.put(p, r, b, value)
            images[j, b, pl.ds(r, SUBS, stride=R), :] = (
                image_ref[j, r, :, at]
                + re * receivers_ref[j, 0, r, :, at]
                + im * receivers_ref[j, 1, r, :, at]
            )

        def done(b, j=j, final=final):
            for a in range(tiles_x):
                p = (j * tiles_x + a) * tiles_y + b
                copies.append(
                    pltpu.make_async_copy(
                        images.at[j, b, pl.ds(a * rows, rows)],
                        buffer_ref.at[
                            owners_ref[0, p], pl.ds(pl.multiple_of(ranks[p] * rows, rows), rows)
                        ],
                        sem.at[p],
                    )
                )
                copies[-1].start()
            if final:
                at = pl.ds(b * LANES, LANES)
                copies.append(
                    pltpu.make_async_copy(
                        last_state.at[:, :, :, at], state_out.at[:, :, :, at], state_sem.at[b]
                    )
                )
                copies[-1].start()

        if j:
            state.halo()
            along_y(state, sides_ref, sums)
        depth_step(state, sums, coefs_ref.at[j], 1, emit, done=done)
    for copy in copies:
        copy.wait()


def output_kernel(source_ref, receivers_ref, out_ref, flat, sems):
    R = source_ref.shape[1]
    blocks = flat.shape[2]

    def body(r, _):
        for b in range(blocks):
            at = slice(b * LANES, (b + 1) * LANES)
            for p in (0, 1):
                flat[0, p, b, pl.ds(r, SUBS, stride=R), :] = source_ref[p, r, :, at]
                flat[1, p, b, pl.ds(r, SUBS, stride=R), :] = receivers_ref[receivers_ref.shape[0] - 1, p, r, :, at]
        return 0

    lax.fori_loop(0, R, body, 0, unroll=4)
    copies = [
        pltpu.make_async_copy(flat.at[:, :, b], out_ref.at[:, :, :, pl.ds(b * LANES, LANES)], sems.at[b])
        for b in range(blocks)
    ]
    for copy in copies:
        copy.start()
    for copy in copies:
        copy.wait()


def volume_kernel(received_ref, out_ref, slots, slot_sem, seats, sems):
    peers, rows, size = seats.shape
    first = pltpu.make_async_copy(received_ref.at[:, pl.ds(rows, 1)], slots, slot_sem)
    first.start()
    copies = []
    for s in range(peers):
        copies.append(
            pltpu.make_async_copy(received_ref.at[s, pl.ds(0, rows)], seats.at[s], sems.at[s])
        )
        copies[-1].start()
    out_ref[...] = jnp.zeros_like(out_ref)
    first.wait()
    for s in range(peers):
        copies[s].wait()
        for i in range(CAP):
            slot = slots[s, 0, i].astype(jnp.int32)

            @pl.when(slot >= 0)
            def _(s=s, i=i, slot=slot):
                out_ref[slot] += seats[s, i * size : (i + 1) * size, :]


def shifted(shard, axis, by):
    peers = lax.axis_size(axis)
    return lax.ppermute(shard, axis, [(i, i + by) for i in range(peers - by)])


def swapped(shard, axis, bits):
    return lax.ppermute(shard, axis, [(i, i ^ bits) for i in range(lax.axis_size(axis))])


def local(fields, vel_tiles, tile_ids, orders, term_weights, phase_rates, owners, image_slots):
    axis = "depth"
    peers = lax.axis_size(axis)
    cells_x, cells_y = fields.shape[3:]
    size = vel_tiles.shape[1]
    steps, tiles_x, tiles_y = tile_ids.shape[1:]
    terms = phase_rates.shape[0]
    R = cells_x // SUBS
    f32 = jnp.float32

    blocks = cells_y // LANES
    assert size == LANES and cells_x % SUBS == 0 and cells_y % LANES == 0

    edge = terms - 1
    sides = lane_sums(cells_y, terms)

    def flat(planes):
        return [pltpu.VMEM((planes, blocks, cells_x, LANES), f32), pltpu.SemaphoreType.DMA((blocks,))]

    def work(planes):
        return [
            pltpu.VMEM((planes, R + 2 * edge, SUBS, cells_y), f32),
            pltpu.VMEM((edge, 2, R + 2 * edge, SUBS, cells_y), f32),
        ]

    planes = (R, SUBS, cells_y)
    padded = (R + 2 * edge, SUBS, cells_y)
    call = partial(pl.pallas_call, compiler_params=PARAMS)
    ext, rows = call(
        rows_kernel,
        out_shape=(pltpu.VMEM((4,) + padded, f32), pltpu.VMEM((2, R + 1) + planes[1:], f32)),
        in_specs=[SMEM] * 2 + [ANY],
        out_specs=(VMEM, VMEM),
        scratch_shapes=flat(4) + [pltpu.SemaphoreType.DMA],
        name="rows",
    )(tile_ids, orders, in_hbm(fields.reshape(4, cells_x, cells_y)))

    def stacked(parts):
        return call(
            stack_kernel,
            out_shape=pltpu.VMEM((len(parts),) + vel_tiles.shape, f32),
            in_specs=[ANY] * len(parts),
            out_specs=VMEM,
            scratch_shapes=[pltpu.SemaphoreType.DMA((len(parts),))],
            name="stack_tiles",
        )(*parts)

    line = [vel_tiles] + [swapped(vel_tiles, axis, 4 * i) for i in range(1, peers // 4 - 1)]
    across = [swapped(vel_tiles, axis, 2)]
    ext, rows, across[0], *line[1:] = lax.optimization_barrier((ext, rows, across[0], *line[1:]))
    across += [swapped(v, axis, 2) for v in line[1:]]
    line.append(swapped(line[-1], axis, 4))
    ext = in_vmem(ext)

    def summed(first):
        return call(
            partial(sums_kernel, first),
            out_shape=pltpu.VMEM((edge, 2) + padded, f32),
            in_specs=[VMEM, VMEM],
            out_specs=VMEM,
            name="first_sums",
        )(ext, sides)

    line[-1], source_sums = lax.optimization_barrier((line[-1], summed(0)))
    across.append(swapped(line[-1], axis, 2))
    across[0], receiver_sums = lax.optimization_barrier((across[0], summed(2)))
    tiles = {0: stacked(line)}
    tiles[1] = swapped(tiles[0], axis, 1)
    tiles[2] = stacked(across)
    tiles[2], rows = lax.optimization_barrier((tiles[2], rows))
    tiles[3] = swapped(tiles[2], axis, 1)
    receiver_up = shifted(rows, axis, 1)
    source_sums, receiver_sums = in_vmem(source_sums), in_vmem(receiver_sums)
    tiles = [in_vmem(tiles[i]) for i in range(4)]
    slow = [pltpu.VMEM((blocks, cells_x, LANES), f32)]
    coefs, states, sent = call(
        partial(first_source_kernel, axis),
        out_shape=(
            pltpu.VMEM((steps, 2 * terms) + planes, f32),
            pltpu.VMEM((steps, 2) + planes, f32),
            pltpu.VMEM((2,) + planes, f32),
        ),
        in_specs=[SMEM] * 4 + [VMEM] * 7,
        out_specs=(VMEM, VMEM, VMEM),
        scratch_shapes=slow + work(2),
        name="first_sources",
    )(tile_ids, orders, term_weights, phase_rates, sides, ext, source_sums, *tiles)
    source_up = shifted(sent, axis, 1)
    coefs, states = in_vmem(coefs), in_vmem(states)
    image = call(
        first_image_kernel,
        out_shape=pltpu.VMEM((steps,) + planes, f32),
        in_specs=[VMEM] * 5,
        out_specs=VMEM,
        scratch_shapes=work(2),
        name="first_images",
    )(sides, ext, receiver_sums, coefs, states)
    image, receiver_up = lax.optimization_barrier((image, receiver_up))
    receivers = in_vmem(
        call(
            partial(receiver_kernel, axis),
            out_shape=pltpu.VMEM((steps, 2) + planes, f32),
            in_specs=[SMEM] * 2 + [ANY] + [VMEM] * 7,
            out_specs=VMEM,
            scratch_shapes=[pltpu.SMEM((SUBS, cells_y), f32), pltpu.SemaphoreType.DMA]
            + slow
            + [pltpu.VMEM((1, 2 * terms) + planes, f32)]
            + work(2),
            name="receiver_ticks",
        )(term_weights, phase_rates, receiver_up, in_vmem(receiver_up), *tiles, sides, coefs)
    )
    extra = SUBS
    buffer, source = call(
        source_kernel,
        out_shape=(
            pltpu.HBM((peers, CAP * size + extra, size), f32),
            pltpu.HBM((2,) + planes, f32),
        ),
        in_specs=[VMEM] * 5 + [SMEM] * 2,
        out_specs=(ANY, ANY),
        scratch_shapes=[
            pltpu.VMEM((steps, blocks, cells_x, LANES), f32),
            pltpu.VMEM((peers, extra, size), f32),
            pltpu.SMEM((peers * CAP,), jnp.int32),
            pltpu.SemaphoreType.DMA((steps * tiles_x * tiles_y,)),
            pltpu.SemaphoreType.DMA,
            pltpu.SemaphoreType.DMA((blocks,)),
            pltpu.VMEM((2,) + planes, f32),
        ]
        + work(2),
        name="source_tick_and_seats",
    )(in_vmem(source_up), coefs, sides, receivers, in_vmem(image), owners, image_slots)
    received = lax.all_to_all(buffer, axis, split_axis=0, concat_axis=0, tiled=True)
    wavefields = pl.pallas_call(
        output_kernel,
        out_shape=jax.ShapeDtypeStruct((2, 2, cells_x, cells_y), f32),
        in_specs=[VMEM, VMEM],
        out_specs=ANY,
        scratch_shapes=[
            pltpu.VMEM((2, 2, blocks, cells_x, LANES), f32),
            pltpu.SemaphoreType.DMA((blocks,)),
        ],
        compiler_params=PARAMS,
        name="wavefields",
    )(source, receivers)
    volume = call(
        volume_kernel,
        out_shape=jax.ShapeDtypeStruct((IMG_SLOTS, size, size), f32),
        in_specs=[ANY],
        out_specs=VMEM,
        scratch_shapes=[
            pltpu.SMEM((peers, 1, size), f32),
            pltpu.SemaphoreType.DMA,
            pltpu.VMEM((peers, CAP * size, size), f32),
            pltpu.SemaphoreType.DMA((peers,)),
        ],
        name="image_volume",
    )(received)
    return volume, wavefields[None]


def solution(mesh):
    placed = (
        P(("groups", "depth"), None, None, None, None),
        P(("groups", "depth"), None, None),
        P(("groups", "depth"), None, None, None),
        P(("groups", "depth"), None),
        P(),
        P(),
        P(("groups", "depth"), None),
        P(("groups", "depth"), None),
    )
    return jax.shard_map(
        local,
        mesh=mesh,
        in_specs=placed,
        out_specs=(
            P(("groups", "depth"), None, None),
            P(("groups", "depth"), None, None, None, None),
        ),
        check_vma=False,
    )
```
